128 devices in a mesh: section: 8 (over z, y_hi), dp: 16 (over x, y_lo, core).
Axes of the slice: x: 4, y: 4 (y_hi: 2, y_lo: 2; y = y_hi * 2 + y_lo), z: 4, core: 2. Of those that a mesh axis runs over, the one named last changes fastest.
Arguments:
- inputs: bfloat16 [4, 1024, 2560], P(None, 'dp'), may hold values from -6 to 6
- cotangent: bfloat16 [4, 1024, 2560], P(None, 'dp'), may hold values from -6 to 6
- weight: bfloat16 [8, 2560, 2560], P('section'), may hold values from -0.125 to 0.125
- gain: float32 [8, 2560], P('section'), may hold values from 0.1 to 1.9
Outputs:
- acts: bfloat16 [8, 4, 1024, 2560], P('section', None, 'dp')
- input_grads: bfloat16 [8, 4, 1024, 2560], P('section', None, 'dp')
- weight_grad: float32 [8, 2560, 2560], P('section', 'dp')
The draws below stay inside these ranges and needn't reach their ends.
All inputs are finite; a program needn't handle non-finite values.
Results may differ from the reference program's by a relative error of at most 0.029.
Values may be sent and summed in bfloat16 or wider, within the bound.
A program may use at most 128 MiB of HBM per device.

```python
import jax
import jax.numpy as jnp
from jax import lax

D = 2560
MICRO = 4
ROWS = 64
TOKENS = 1024
LAYERS = 8
N_SECTION = 8
N_DP = 16


def levels(rng, shape, pieces, least, largest):
    def one(position, shards_of):
        heights = jax.random.uniform(jax.random.fold_in(jax.random.fold_in(rng, 6), position), (shards_of,), jnp.float32, least / len(pieces), largest / len(pieces))
        return jnp.repeat(jnp.exp(heights), shape[position] // shards_of).reshape((-1,) + (1,) * (len(shape) - position - 1))

    level = one(*pieces[0])
    for cut in pieces[1:]:
        level = level * one(*cut)
    return level


def scatter_about(rng, extent, scale, most, shards=(), held_as=jnp.bfloat16):
    level = levels(rng, extent, shards, -0.22, 0.18) if shards else 1.0
    array = jax.random.normal(rng, extent, jnp.float32) * scale * level
    return jnp.minimum(jnp.maximum(array, -most), most).astype(held_as)


def setup_inputs(seed: int = 0) -> dict:
    arg_keys = jax.random.split(jax.random.key(seed), 5)
    return {
        "inputs": scatter_about(arg_keys[0], (MICRO, TOKENS, D), 1.0, 6.0, ((1, 16),)),
        "cotangent": scatter_about(arg_keys[1], (MICRO, TOKENS, D), 1.0, 6.0, ((1, 16),)),
        "weight": scatter_about(arg_keys[2], (LAYERS, D, D), D ** -0.5, 0.125, ((0, 8),)),
        "gain": jnp.clip(1.0 + 0.18 * jax.random.normal(arg_keys[3], (LAYERS, D), jnp.float32), 0.1, 1.9),
    }


EPS = 1e-05

def norm_parts(x, g):
    xf = x.astype(jnp.float32)
    r = lax.rsqrt(lax.optimization_barrier(jnp.mean(xf * xf, -1, keepdims=True)) + EPS)
    n = (xf * r * g).astype(jnp.bfloat16)
    return (xf, r, n)

def silu_slope(a):
    s = jax.nn.sigmoid(a)
    return s * (1.0 + a * (1.0 - s))

def reference(inputs, cotangent, weight, gain):
    width = inputs.shape[2]
    x = inputs.reshape(-1, width)
    saved = []
    outs = []
    for layer in range(N_SECTION):
        saved.append(x)
        xf, r, n = norm_parts(x, gain[layer])
        a = jnp.dot(n, weight[layer], preferred_element_type=jnp.float32)
        x = (xf + jax.nn.silu(a)).astype(jnp.bfloat16)
        outs.append(x)
    d = cotangent.reshape(-1, width)
    grads = [None] * N_SECTION
    wgrads = [None] * N_SECTION
    scale = (MICRO * TOKENS) ** (-0.5)
    for layer in reversed(range(N_SECTION)):
        x_in = saved[layer]
        xf, r, n = norm_parts(x_in, gain[layer])
        a = jnp.dot(n, weight[layer], preferred_element_type=jnp.float32)
        s = (d.astype(jnp.float32) * silu_slope(a)).astype(jnp.bfloat16)
        n_groups = n.reshape(MICRO, N_DP, ROWS, width).astype(jnp.float32)
        s_groups = s.reshape(MICRO, N_DP, ROWS, width).astype(jnp.float32)

        def group_part(pair):
            return jnp.einsum('mrd,mre->de', pair[0], pair[1]).astype(jnp.bfloat16).astype(jnp.float32)
        parts = lax.map(group_part, (jnp.swapaxes(n_groups, 0, 1), jnp.swapaxes(s_groups, 0, 1)))
        wgrads[layer] = lax.optimization_barrier(jnp.sum(parts, axis=0)) * scale
        e = lax.dot_general(s, weight[layer], (((1,), (1,)), ((), ())), preferred_element_type=jnp.float32)
        h = gain[layer] * e
        dx = d.astype(jnp.float32) + r * h - xf * r ** 3 * lax.optimization_barrier(jnp.mean(xf * h, -1, keepdims=True))
        d = dx.astype(jnp.bfloat16)
        grads[layer] = d
    shape = (N_SECTION, MICRO, TOKENS, width)
    return (jnp.stack(outs).reshape(shape), jnp.stack(grads).reshape(shape), jnp.stack(wgrads))
```

```python
import functools

import jax
import jax.numpy as jnp
from jax import lax
from jax.experimental import pallas as pl
from jax.experimental.pallas import tpu as pltpu
from jax.sharding import PartitionSpec as P

EPS = 1e-05
MESH = pl.DeviceIdType.MESH
BF16, F32 = jnp.bfloat16, jnp.float32

CHUNK = 64
PIECES = 5
SPLIT = 1408


def kernel(
    x_hbm, d_hbm, w_hbm, gain, acts, grads, wgrad,
    w_v, wt_v, xs, ds_in, slope, rinv, acc, n2, s2, nt, part, got_a1, got_a2, got_a3, got_b1, got_b2, got_b3,
    w_sem, f_send, f_recv, b_send, b_recv, n_send, n_recv, s_send, s_recv, r_send, r_recv,
):
    total, width = xs.shape
    count = total // CHUNK
    piece = width // PIECES
    share = wgrad.shape[0]
    section, dp = lax.axis_index("section"), lax.axis_index("dp")
    sections = lax.axis_size("section")
    x, y, core = dp // 4, (dp // 2) % 2, dp % 2
    first, last = section == 0, section == sections - 1

    def at(x_to, y_to, core_to):
        return (section, x_to * 4 + y_to * 2 + core_to)

    after, before = (section + 1, dp), (section - 1, dp)
    twin = at(x, y, 1 - core)
    right, left, across = at((x + 1) % 4, y, core), at((x + 3) % 4, y, core), at(x, 1 - y, core)

    def local(source, target, sem):
        return pltpu.make_async_copy(source, target, sem)

    def remote(source, target, send, recv, device):
        return pltpu.make_async_remote_copy(
            src_ref=source, dst_ref=target, send_sem=send, recv_sem=recv, device_id=device, device_id_type=MESH
        )

    def cols(p):
        return slice(p * piece, (p + 1) * piece)

    def rows_of(m):
        return pl.ds(pl.multiple_of(m * CHUNK, CHUNK), CHUNK)

    for p in range(PIECES):
        local(w_hbm.at[cols(p), :], w_v.at[cols(p), :], w_sem.at[p]).start()

    def fetch(source, target, sems):
        @pl.loop(0, count)
        def _(m):
            for p in range(PIECES):
                local(source.at[rows_of(m), cols(p)], target.at[rows_of(m), cols(p)], sems.at[m, p]).start()

    @pl.when(first)
    def _():
        fetch(x_hbm, xs, f_recv)

    @pl.when(last)
    def _():
        fetch(d_hbm, ds_in, b_recv)

    barrier = pltpu.get_barrier_semaphore()
    for device in (twin, right, left, across):
        pl.semaphore_signal(barrier, inc=1, device_id=device, device_id_type=MESH)

    @pl.when(section > 0)
    def _():
        pl.semaphore_signal(barrier, inc=1, device_id=before, device_id_type=MESH)

    @pl.when(section < sections - 1)
    def _():
        pl.semaphore_signal(barrier, inc=1, device_id=after, device_id_type=MESH)

    pl.semaphore_wait(barrier, 4 + (section > 0).astype(jnp.int32) + (section < sections - 1).astype(jnp.int32))

    def turn_weight():
        tile = 256

        @pl.loop(0, width // tile)
        def _(i):
            i = pl.ds(pl.multiple_of(i * tile, tile), tile)
            for j in range(0, width, tile):
                wt_v[j : j + tile, i] = w_v[i, j : j + tile].T

    def await_weight():
        for p in range(PIECES):
            local(w_hbm.at[cols(p), :], w_v.at[cols(p), :], w_sem.at[p]).wait()

    early = section >= sections // 2

    @pl.when(early)
    def _():
        await_weight()
        turn_weight()

    def add_product(lhs, rhs, p):
        tile = 512
        for j in range(0, width, tile):
            term = jnp.dot(lhs, rhs[cols(p), j : j + tile], preferred_element_type=F32)
            if p == 0:
                acc[:, j : j + tile] = term
            else:
                acc[:, j : j + tile] += term

    def lane_sum(values):
        out = values[:, :128]
        for j in range(128, values.shape[1], 128):
            out = out + values[:, j : j + 128]
        return out

    def forward(m, carry):
        rows = rows_of(m)
        squares = None
        for p in range(PIECES):
            local(xs.at[rows, cols(p)], xs.at[rows, cols(p)], f_recv.at[m, p]).wait()
            if p >= 0:

                @pl.when(jnp.logical_and(m == 0, jnp.logical_not(early)))
                def _():
                    local(w_hbm.at[cols(p), :], w_v.at[cols(p), :], w_sem.at[p]).wait()

            xf = xs[rows, cols(p)].astype(F32)
            term = lane_sum(xf * xf)
            squares = term if squares is None else squares + term
            add_product((xf * gain[:, cols(p)]).astype(BF16), w_v, p)
        r = lax.rsqrt(jnp.sum(squares, -1, keepdims=True) * (1.0 / width) + EPS)
        rinv[rows, :] = jnp.broadcast_to(r, (CHUNK, 128))
        for p in range(PIECES):
            a = acc[:, cols(p)] * r
            xf = xs[rows, cols(p)].astype(F32)
            sig = jax.nn.sigmoid(a)
            acts[rows, cols(p)] = (xf + a * sig).astype(BF16)

            @pl.when(section < sections - 1)
            def _():
                remote(
                    acts.at[rows, cols(p)], xs.at[rows, cols(p)], f_send.at[m, p], f_recv.at[m, p], after
                ).start()

            slope[rows, cols(p)] = sig * (1.0 + a * (1.0 - sig))
            n2[rows, cols(p)] = (xf * r * gain[:, cols(p)]).astype(BF16)
        remote(n2.at[rows, :], n2.at[pl.ds(pl.multiple_of(total + m * CHUNK, CHUNK), CHUNK), :], n_send.at[m], n_recv.at[m], twin).start()
        return carry

    lax.fori_loop(0, count, forward, 0)

    def turn_normed():
        tile = 256

        @pl.loop(0, count)
        def _(m):
            other = pl.ds(pl.multiple_of(total + m * CHUNK, CHUNK), CHUNK)
            remote(n2.at[rows_of(m), :], n2.at[other, :], n_send.at[m], n_recv.at[m], twin).wait_recv()

        @pl.loop(0, width // tile)
        def _(i):
            i = pl.ds(pl.multiple_of(i * tile, tile), tile)
            nt[i, :] = n2[:, i].T

    @pl.when(jnp.logical_not(early))
    def _():
        turn_weight()
        turn_normed()

    def backward(m, carry):
        rows = rows_of(m)
        for p in range(PIECES):
            local(ds_in.at[rows, cols(p)], ds_in.at[rows, cols(p)], b_recv.at[m, p]).wait()
            s = (ds_in[rows, cols(p)].astype(F32) * slope[rows, cols(p)]).astype(BF16)
            s2[rows, cols(p)] = s
            add_product(s, wt_v, p)
        remote(s2.at[rows, :], s2.at[pl.ds(pl.multiple_of(total + m * CHUNK, CHUNK), CHUNK), :], s_send.at[m], s_recv.at[m], twin).start()
        dots = None
        for p in range(PIECES):
            h = acc[:, cols(p)] * gain[:, cols(p)]
            acc[:, cols(p)] = h
            term = lane_sum(xs[rows, cols(p)].astype(F32) * h)
            dots = term if dots is None else dots + term
        r = rinv[rows, :1]
        scale = r * r * r * (jnp.sum(dots, -1, keepdims=True) * (1.0 / width))
        for p in range(PIECES):
            out = ds_in[rows, cols(p)].astype(F32) + r * acc[:, cols(p)] - xs[rows, cols(p)].astype(F32) * scale
            grads[rows, cols(p)] = out.astype(BF16)

            @pl.when(section > 0)
            def _():
                remote(
                    grads.at[rows, cols(p)], ds_in.at[rows, cols(p)], b_send.at[m, p], b_recv.at[m, p], before
                ).start()

        return carry

    lax.fori_loop(0, count, backward, 0)

    @pl.when(early)
    def _():
        turn_normed()

    @pl.loop(0, count)
    def _(m):
        other = pl.ds(pl.multiple_of(total + m * CHUNK, CHUNK), CHUNK)
        remote(s2.at[rows_of(m), :], s2.at[other, :], s_send.at[m], s_recv.at[m], twin).wait_recv()

    def block(x_to, y_to):
        return x_to * 2 + y_to

    def make_block(b):
        rows = pl.ds(pl.multiple_of((b * 2 + core) * share, 32), share)
        tile = 512

        @pl.loop(0, width // tile)
        def _(j):
            j = pl.ds(pl.multiple_of(j * tile, tile), tile)
            part[b, :, j] = jnp.dot(nt[rows, :], s2[:, j], preferred_element_type=F32).astype(BF16)

    far, plus, minus = (x + 2) % 4, (x + 1) % 4, (x + 3) % 4
    here, there = y, 1 - y
    a_cols, b_cols = slice(0, SPLIT), slice(SPLIT, width)
    half = share // 2
    copies = []

    def send(source, target, device):
        k = len(copies)
        copy = remote(source, target, r_send.at[k], r_recv.at[k], device)
        copy.start()
        copies.append(copy)
        return copy

    make_block(block(far, 0))
    a1_right = send(part.at[block(far, 0), :, a_cols], got_a1.at[0], right)
    make_block(block(far, 1))
    a1_left = send(part.at[block(far, 1), :, a_cols], got_a1.at[1], left)
    b1 = [send(part.at[block(far, there), :, b_cols], got_b1.at[far], across)]
    make_block(block(plus, there))
    b1.append(send(part.at[block(plus, there), :, b_cols], got_b1.at[plus], across))
    make_block(block(plus, here))
    a2_right = [send(part.at[block(plus, 1), :, a_cols], got_a2.at[0, 1], right)]
    make_block(block(minus, there))
    b1.append(send(part.at[block(minus, there), :, b_cols], got_b1.at[minus], across))
    make_block(block(minus, here))
    a2_left = [send(part.at[block(minus, 0), :, a_cols], got_a2.at[1, 0], left)]
    make_block(block(x, there))
    b1.append(send(part.at[block(x, there), :, b_cols], got_b1.at[x], across))
    make_block(block(x, here))

    def add_into(b, r0, r1, columns, other):
        for r in range(r0, r1, 16):
            part[b, r : r + 16, columns] = (
                part[b, r : r + 16, columns].astype(F32) + other[r - r0 : r - r0 + 16, :].astype(F32)
            ).astype(BF16)

    a1_right.wait_recv()
    add_into(block(plus, 0), 0, share, a_cols, got_a1.at[0])
    a2_right.append(send(part.at[block(plus, 0), :, a_cols], got_a2.at[0, 0], right))
    a1_left.wait_recv()
    add_into(block(minus, 1), 0, share, a_cols, got_a1.at[1])
    a2_left.append(send(part.at[block(minus, 1), :, a_cols], got_a2.at[1, 1], left))

    b1[0].wait_recv()
    add_into(block(far, here), 0, share, b_cols, got_b1.at[far])
    b2_right = send(part.at[block(far, here), :half, b_cols], got_b2.at[0], right)
    b2_left = send(part.at[block(far, here), half:, b_cols], got_b2.at[1], left)
    b1[1].wait_recv()
    add_into(block(plus, here), 0, share, b_cols, got_b1.at[plus])
    b3_right = [send(part.at[block(plus, here), half:, b_cols], got_b3.at[0, half:], right)]
    b1[2].wait_recv()
    add_into(block(minus, here), 0, share, b_cols, got_b1.at[minus])
    b3_left = [send(part.at[block(minus, here), :half, b_cols], got_b3.at[1, :half], left)]

    for copy in a2_right + a2_left:
        copy.wait_recv()
    for r in range(0, share, 16):
        rr = slice(r, r + 16)
        part[block(x, there), rr, a_cols] = (
            part[block(x, there), rr, a_cols].astype(F32)
            + got_a2[0, there, rr, :].astype(F32)
            + got_a2[1, there, rr, :].astype(F32)
        ).astype(BF16)
    a3 = send(part.at[block(x, there), :, a_cols], got_a3, across)

    b2_right.wait_recv()
    add_into(block(plus, here), 0, half, b_cols, got_b2.at[0])
    b3_right.append(send(part.at[block(plus, here), :half, b_cols], got_b3.at[0, :half], right))
    b2_left.wait_recv()
    add_into(block(minus, here), half, share, b_cols, got_b2.at[1])
    b3_left.append(send(part.at[block(minus, here), half:, b_cols], got_b3.at[1, half:], left))
    b1[3].wait_recv()

    norm = float(4096) ** (-0.5)
    for copy in b3_right + b3_left:
        copy.wait_recv()
    for r in range(0, share, 16):
        rr = slice(r, r + 16)
        wgrad[rr, b_cols] = norm * (
            part[block(x, here), rr, b_cols].astype(F32)
            + got_b1[x, rr, :].astype(F32)
            + got_b3[0, rr, :].astype(F32)
            + got_b3[1, rr, :].astype(F32)
        )
    a3.wait_recv()
    for r in range(0, share, 16):
        rr = slice(r, r + 16)
        wgrad[rr, a_cols] = norm * (
            part[block(x, here), rr, a_cols].astype(F32)
            + got_a2[0, here, rr, :].astype(F32)
            + got_a2[1, here, rr, :].astype(F32)
            + got_a3[rr, :].astype(F32)
        )

    for copy in copies:
        copy.wait_send()

    @pl.loop(0, count)
    def _(m):
        rows = rows_of(m)
        other = pl.ds(pl.multiple_of(total + m * CHUNK, CHUNK), CHUNK)
        remote(n2.at[rows, :], n2.at[other, :], n_send.at[m], n_recv.at[m], twin).wait_send()
        remote(s2.at[rows, :], s2.at[other, :], s_send.at[m], s_recv.at[m], twin).wait_send()
        for p in range(PIECES):

            @pl.when(section < sections - 1)
            def _():
                remote(
                    acts.at[rows, cols(p)], xs.at[rows, cols(p)], f_send.at[m, p], f_recv.at[m, p], after
                ).wait_send()

            @pl.when(section > 0)
            def _():
                remote(
                    grads.at[rows, cols(p)], ds_in.at[rows, cols(p)], b_send.at[m, p], b_recv.at[m, p], before
                ).wait_send()


def body(inputs, cotangent, weight, gain):
    micro, tokens, width = inputs.shape
    total = micro * tokens
    share = width // lax.axis_size("dp")
    count = total // CHUNK
    rest = width - SPLIT
    half = share // 2
    vmem, dma = pltpu.VMEM, pltpu.SemaphoreType.DMA
    acts, grads, wgrad = pl.pallas_call(
        kernel,
        out_shape=(
            jax.ShapeDtypeStruct((total, width), BF16),
            jax.ShapeDtypeStruct((total, width), BF16),
            jax.ShapeDtypeStruct((share, width), F32),
        ),
        in_specs=[pl.BlockSpec(memory_space=pl.ANY)] * 3 + [pl.BlockSpec(memory_space=vmem)],
        out_specs=[pl.BlockSpec(memory_space=vmem)] * 3,
        scratch_shapes=[
            vmem((width, width), BF16),
            vmem((width, width), BF16),
            vmem((total, width), BF16),
            vmem((total, width), BF16),
            vmem((total, width), F32),
            vmem((total, 128), F32),
            vmem((CHUNK, width), F32),
            vmem((2 * total, width), BF16),
            vmem((2 * total, width), BF16),
            vmem((width, 2 * total), BF16),
            vmem((8, share, width), BF16),
            vmem((2, share, SPLIT), BF16),
            vmem((2, 2, share, SPLIT), BF16),
            vmem((share, SPLIT), BF16),
            vmem((4, share, rest), BF16),
            vmem((2, half, rest), BF16),
            vmem((2, share, rest), BF16),
            dma((PIECES,)),
            dma((count, PIECES)),
            dma((count, PIECES)),
            dma((count, PIECES)),
            dma((count, PIECES)),
            dma((count,)),
            dma((count,)),
            dma((count,)),
            dma((count,)),
            dma((17,)),
            dma((17,)),
        ],
        compiler_params=pltpu.CompilerParams(
            collective_id=0, has_side_effects=True, vmem_limit_bytes=60 * 1024 * 1024
        ),
    )(inputs.reshape(total, width), cotangent.reshape(total, width), weight[0], gain)
    shape = (1, micro, tokens, width)
    return (acts.reshape(shape), grads.reshape(shape), wgrad[None])


def solution(mesh):
    in_specs = (
        P(None, "dp", None),
        P(None, "dp", None),
        P("section", None, None),
        P("section", None),
    )
    out_specs = (
        P("section", None, "dp", None),
        P("section", None, "dp", None),
        P("section", "dp", None),
    )
    return jax.shard_map(body, mesh=mesh, in_specs=in_specs, out_specs=out_specs, check_vma=False)
```

```python
import jax
import jax.numpy as jnp
from jax import lax
from jax.experimental import pallas as pl
from jax.experimental.pallas import tpu as pltpu
from jax.sharding import PartitionSpec as P

EPS = 1e-05
MESH = pl.DeviceIdType.MESH
BF16, F32 = jnp.bfloat16, jnp.float32

CHUNK = 16
PIECES = 5
GROUP = 64
AHEAD = 7
QUARTERS = 4


def kernel(
    x_hbm, d_hbm, w_hbm, gain, acts_out, grads_out, wgrad_out,
    w_v, wt_v, xs, ds_in, acts, grads, pre, rinv, acc, normed, nx, nt, sx, total_p,
    to_twin, from_twin, to_across, from_across, wgrad,
    w_sem, x_sem, d_sem, out_sem, f_send, f_recv, b_send, b_recv, n_send, n_recv, s_send, s_recv,
    t_send, t_recv, y_send, y_recv,
):
    total, width = xs.shape
    count = total // CHUNK
    piece = width // PIECES
    window = nt.shape[0]
    share = wgrad.shape[0]
    quarter = width // QUARTERS
    ways = window // share
    per_group = GROUP // CHUNK
    groups = total // GROUP
    deep = 4 * GROUP
    section, dp = lax.axis_index("section"), lax.axis_index("dp")
    sections = lax.axis_size("section")
    x, y, core = dp // 4, (dp // 2) % 2, dp % 2
    first, last = section == 0, section == sections - 1
    early = section >= sections // 2

    def at(x_to, y_to, core_to):
        return (section, x_to * 4 + y_to * 2 + core_to)

    after, before = (section + 1, dp), (section - 1, dp)
    twin, across = at(x, y, 1 - core), at(x, 1 - y, core)
    steps = (1, 3, 2)
    others = [(x + step) % 4 for step in steps]

    def local(source, target, sem):
        return pltpu.make_async_copy(source, target, sem)

    def remote(source, target, send, recv, device):
        return pltpu.make_async_remote_copy(
            src_ref=source, dst_ref=target, send_sem=send, recv_sem=recv, device_id=device, device_id_type=MESH
        )

    def cols(p):
        return slice(p * piece, (p + 1) * piece)

    def rows_of(m):
        return pl.ds(pl.multiple_of(m * CHUNK, CHUNK), CHUNK)

    def slot(m, source):
        start = (m // per_group) * deep + source * GROUP + (m % per_group) * CHUNK
        return pl.ds(pl.multiple_of(start, CHUNK), CHUNK)

    def fetch_x(p):
        return local(x_hbm.at[:, cols(p)], xs.at[:, cols(p)], x_sem.at[p])

    def fetch_d(p):
        return local(d_hbm.at[:, cols(p)], ds_in.at[:, cols(p)], d_sem.at[p])

    def fetch_w(p):
        return local(w_hbm.at[cols(p), :], w_v.at[cols(p), :], w_sem.at[p])

    def push_acts(m, p):
        here = (rows_of(m), cols(p))
        return remote(acts.at[here], xs.at[here], f_send.at[m, p], f_recv.at[m, p], after)

    def push_grads(m, p):
        here = (rows_of(m), cols(p))
        return remote(grads.at[here], ds_in.at[here], b_send.at[m, p], b_recv.at[m, p], before)

    def push_normed(m, k):
        part = pl.ds(pl.multiple_of(others[k] * window, 128), window)
        return remote(
            normed.at[rows_of(m), part], nx.at[slot(m, x), :], n_send.at[k, m], n_recv.at[k, m], at(others[k], y, core)
        )

    def push_s(m, k):
        here = sx.at[slot(m, x), :]
        return remote(here, here, s_send.at[k, m], s_recv.at[k, m], at(others[k], y, core))

    def keep_acts(m):
        return local(acts.at[rows_of(m), :], acts_out.at[rows_of(m), :], out_sem.at[0, m])

    def keep_grads(m):
        return local(grads.at[rows_of(m), :], grads_out.at[rows_of(m), :], out_sem.at[1, m])

    @pl.when(first)
    def _():
        for p in range(PIECES):
            fetch_x(p).start()

    for p in range(PIECES):
        fetch_w(p).start()

    @pl.when(last)
    def _():
        for p in range(PIECES):
            fetch_d(p).start()

    barrier = pltpu.get_barrier_semaphore()
    for device in [twin, across] + [at(other, y, core) for other in others]:
        pl.semaphore_signal(barrier, inc=1, device_id=device, device_id_type=MESH)

    @pl.when(section > 0)
    def _():
        pl.semaphore_signal(barrier, inc=1, device_id=before, device_id_type=MESH)

    @pl.when(section < sections - 1)
    def _():
        pl.semaphore_signal(barrier, inc=1, device_id=after, device_id_type=MESH)

    pl.semaphore_wait(barrier, 5 + (section > 0).astype(jnp.int32) + (section < sections - 1).astype(jnp.int32))

    def turn_weight():
        tile = 256

        @pl.loop(0, width // tile)
        def _(i):
            i = pl.ds(pl.multiple_of(i * tile, tile), tile)
            for j in range(0, width, tile):
                wt_v[j : j + tile, i] = w_v[i, j : j + tile].T

    def turn_normed():
        for k in range(3):

            @pl.loop(0, count)
            def _(m):
                push_normed(m, k).wait_recv()

        @pl.loop(0, groups)
        def _(g):
            g = pl.ds(pl.multiple_of(g * deep, deep), deep)
            nt[:, g] = nx[g, :].T

        @pl.loop(0, window // 16)
        def _(i):
            i = pl.ds(pl.multiple_of(i * 16, 16), 16)
            total_p[i, :] = jnp.zeros((16, width), F32)

    def await_group(g):
        for k in range(3):
            for i in range(per_group):
                push_s(g * per_group + i, k).wait_recv()

    def add_group(g):
        await_group(g)
        g = pl.ds(pl.multiple_of(g * deep, deep), deep)
        tile = 512

        @pl.loop(0, width // tile)
        def _(j):
            j = pl.ds(pl.multiple_of(j * tile, tile), tile)
            total_p[:, j] += jnp.dot(nt[:, g], sx[g, j], preferred_element_type=F32)

    @pl.when(early)
    def _():
        for p in range(PIECES):
            fetch_w(p).wait()
        turn_weight()

    def add_product(lhs, rhs, p):
        tile = 512
        for j in range(0, width, tile):
            term = jnp.dot(lhs, rhs[cols(p), j : j + tile], preferred_element_type=F32)
            if p == 0:
                acc[:, j : j + tile] = term
            else:
                acc[:, j : j + tile] += term

    def lane_sum(values):
        out = values[:, :128]
        for j in range(128, values.shape[1], 128):
            out = out + values[:, j : j + 128]
        return out

    def forward(m):
        rows = rows_of(m)
        squares = None
        for p in range(PIECES):

            @pl.when(section > 0)
            def _():
                local(xs.at[rows, cols(p)], xs.at[rows, cols(p)], f_recv.at[m, p]).wait()

            @pl.when(jnp.logical_and(m == 0, first))
            def _():
                fetch_x(p).wait()

            @pl.when(jnp.logical_and(m == 0, jnp.logical_not(early)))
            def _():
                fetch_w(p).wait()

            xf = xs[rows, cols(p)].astype(F32)
            term = lane_sum(xf * xf)
            squares = term if squares is None else squares + term
            add_product((xf * gain[:, cols(p)]).astype(BF16), w_v, p)
        r = lax.rsqrt(jnp.sum(squares, -1, keepdims=True) * (1.0 / width) + EPS)
        for p in range(PIECES):
            a = acc[:, cols(p)] * r
            pre[rows, cols(p)] = a
            acts[rows, cols(p)] = (xs[rows, cols(p)].astype(F32) + a * jax.nn.sigmoid(a)).astype(BF16)

            @pl.when(section < sections - 1)
            def _():
                push_acts(m, p).start()

        keep_acts(m).start()
        rinv[rows, :] = jnp.broadcast_to(r, (CHUNK, 128))
        for p in range(PIECES):
            normed[rows, cols(p)] = (xs[rows, cols(p)].astype(F32) * r * gain[:, cols(p)]).astype(BF16)
        nx[slot(m, x), :] = normed[rows, pl.ds(pl.multiple_of(x * window, 128), window)]
        for k in range(3):
            push_normed(m, k).start()

    def backward(m):
        rows = rows_of(m)
        dots = None
        for p in range(PIECES):
            a = pre[rows, cols(p)]
            sig = jax.nn.sigmoid(a)
            slope = sig * (1.0 + a * (1.0 - sig))

            @pl.when(section < sections - 1)
            def _():
                local(ds_in.at[rows, cols(p)], ds_in.at[rows, cols(p)], b_recv.at[m, p]).wait()

            @pl.when(jnp.logical_and(m == 0, last))
            def _():
                fetch_d(p).wait()

            s = (ds_in[rows, cols(p)].astype(F32) * slope).astype(BF16)
            sx[slot(m, x), cols(p)] = s
            term = lane_sum(s.astype(F32) * a)
            dots = term if dots is None else dots + term
            add_product(s, wt_v, p)
        r = rinv[rows, :1]
        scale = r * r * (jnp.sum(dots, -1, keepdims=True) * (1.0 / width))
        for p in range(PIECES):
            out = (
                ds_in[rows, cols(p)].astype(F32)
                + r * (gain[:, cols(p)] * acc[:, cols(p)])
                - xs[rows, cols(p)].astype(F32) * scale
            )
            grads[rows, cols(p)] = out.astype(BF16)

            @pl.when(section > 0)
            def _():
                push_grads(m, p).start()

        for k in range(3):
            push_s(m, k).start()
        keep_grads(m).start()

    behind = sections - 1 - section
    warm = jnp.minimum(count, AHEAD * behind + (behind > 0).astype(jnp.int32))

    @pl.loop(0, 2 * count)
    def _(i):
        @pl.when(i < count)
        def _():
            forward(i)

        @pl.when(jnp.logical_and(i == count - 1, jnp.logical_not(early)))
        def _():
            turn_weight()
            turn_normed()

        m = i - warm

        @pl.when(jnp.logical_and(m >= 0, m < count))
        def _():
            backward(m)

        done = m // per_group - 1

        @pl.when(jnp.logical_and(jnp.logical_not(early), jnp.logical_and(m % per_group == per_group - 1, done >= 0)))
        def _():
            add_group(done)

    @pl.when(early)
    def _():
        turn_normed()

        @pl.loop(0, groups - 1)
        def _(g):
            add_group(g)

    await_group(groups - 1)
    tail = slice((groups - 1) * deep, groups * deep)

    def quarter_of(q):
        return pl.ds(pl.multiple_of(q * quarter, 128), quarter)

    def finished(y_to, core_to, q):
        rows = pl.ds(pl.multiple_of((y_to * 2 + core_to) * share, 32), share)
        return total_p[rows, q] + jnp.dot(nt[rows, tail], sx[tail, q], preferred_element_type=F32)

    def push_twin(k, q):
        return remote(
            to_twin.at[k, :, quarter_of(q)], from_twin.at[k, :, quarter_of(q)], t_send.at[k, q], t_recv.at[k, q], twin
        )

    def push_across(q):
        return remote(
            to_across.at[:, quarter_of(q)], from_across.at[:, quarter_of(q)], y_send.at[q], y_recv.at[q], across
        )

    def keep_wgrad(q):
        return local(wgrad.at[:, quarter_of(q)], wgrad_out.at[:, quarter_of(q)], out_sem.at[2, q])

    norm = float(4096) ** (-0.5)

    @pl.loop(0, QUARTERS)
    def _(q):
        to_twin[0, :, quarter_of(q)] = finished(1 - y, 1 - core, quarter_of(q)).astype(BF16)
        push_twin(0, q).start()

    @pl.loop(0, QUARTERS)
    def _(q):
        value = finished(1 - y, core, quarter_of(q))
        push_twin(0, q).wait_recv()
        to_across[:, quarter_of(q)] = (value + from_twin[0, :, quarter_of(q)].astype(F32)).astype(BF16)
        push_across(q).start()

    @pl.loop(0, QUARTERS)
    def _(q):
        to_twin[1, :, quarter_of(q)] = finished(y, 1 - core, quarter_of(q)).astype(BF16)
        push_twin(1, q).start()

    @pl.loop(0, QUARTERS)
    def _(q):
        value = finished(y, core, quarter_of(q))
        push_twin(1, q).wait_recv()
        wgrad[:, quarter_of(q)] = value + from_twin[1, :, quarter_of(q)].astype(F32)

    @pl.loop(0, QUARTERS)
    def _(q):
        push_across(q).wait_recv()
        wgrad[:, quarter_of(q)] = norm * (wgrad[:, quarter_of(q)] + from_across[:, quarter_of(q)].astype(F32))
        keep_wgrad(q).start()

    @pl.loop(0, QUARTERS)
    def _(q):
        push_twin(0, q).wait_send()
        push_twin(1, q).wait_send()
        push_across(q).wait_send()

    @pl.loop(0, count)
    def _(m):
        for k in range(3):
            push_normed(m, k).wait_send()
            push_s(m, k).wait_send()
        keep_acts(m).wait()
        keep_grads(m).wait()
        for p in range(PIECES):

            @pl.when(section < sections - 1)
            def _():
                push_acts(m, p).wait_send()

            @pl.when(section > 0)
            def _():
                push_grads(m, p).wait_send()

    @pl.loop(0, QUARTERS)
    def _(q):
        keep_wgrad(q).wait()


def place(acts_in, grads_in, wgrad_in, acts, grads, wgrad, held, held_wide, in_sems, out_sems):
    parts = 4
    loads, stores = [], []
    arrays = ((acts_in, held.at[0], acts), (grads_in, held.at[1], grads), (wgrad_in, held_wide, wgrad))
    for k, (source, middle, target) in enumerate(arrays):
        step = source.shape[0] // parts
        for i in range(parts):
            rows = slice(i * step, (i + 1) * step)
            loads.append(pltpu.make_async_copy(source.at[rows, :], middle.at[rows, :], in_sems.at[k, i]))
            stores.append(pltpu.make_async_copy(middle.at[rows, :], target.at[rows, :], out_sems.at[k, i]))
    for load in loads:
        load.start()
    for load, store in zip(loads, stores):
        load.wait()
        store.start()
    for store in stores:
        store.wait()


def body(inputs, cotangent, weight, gain):
    micro, tokens, width = inputs.shape
    total = micro * tokens
    share = width // lax.axis_size("dp")
    window = 4 * share
    count = total // CHUNK
    vmem, dma = pltpu.VMEM, pltpu.SemaphoreType.DMA
    anywhere = pl.BlockSpec(memory_space=pl.ANY)
    shapes = (
        jax.ShapeDtypeStruct((total, width), BF16),
        jax.ShapeDtypeStruct((total, width), BF16),
        jax.ShapeDtypeStruct((share, width), F32),
    )
    results = pl.pallas_call(
        kernel,
        out_shape=shapes,
        in_specs=[anywhere] * 3 + [pl.BlockSpec(memory_space=vmem)],
        out_specs=[anywhere] * 3,
        scratch_shapes=[
            vmem((width, width), BF16),
            vmem((width, width), BF16),
            vmem((total, width), BF16),
            vmem((total, width), BF16),
            vmem((total, width), BF16),
            vmem((total, width), BF16),
            vmem((total, width), F32),
            vmem((total, 128), F32),
            vmem((CHUNK, width), F32),
            vmem((total, width), BF16),
            vmem((4 * total, window), BF16),
            vmem((window, 4 * total), BF16),
            vmem((4 * total, width), BF16),
            vmem((window, width), F32),
            vmem((2, share, width), BF16),
            vmem((2, share, width), BF16),
            vmem((share, width), BF16),
            vmem((share, width), BF16),
            vmem((share, width), F32),
            dma((PIECES,)),
            dma((PIECES,)),
            dma((PIECES,)),
            dma((3, count)),
            dma((count, PIECES)),
            dma((count, PIECES)),
            dma((count, PIECES)),
            dma((count, PIECES)),
            dma((3, count)),
            dma((3, count)),
            dma((3, count)),
            dma((3, count)),
            dma((2, QUARTERS)),
            dma((2, QUARTERS)),
            dma((QUARTERS,)),
            dma((QUARTERS,)),
        ],
        compiler_params=pltpu.CompilerParams(
            collective_id=0, has_side_effects=True, vmem_limit_bytes=62 * 1024 * 1024
        ),
    )(inputs.reshape(total, width), cotangent.reshape(total, width), weight[0], gain)
    acts, grads, wgrad = pl.pallas_call(
        place,
        out_shape=shapes,
        in_specs=[anywhere] * 3,
        out_specs=[anywhere] * 3,
        scratch_shapes=[vmem((2, total, width), BF16), vmem((share, width), F32), dma((3, 4)), dma((3, 4))],
        compiler_params=pltpu.CompilerParams(vmem_limit_bytes=62 * 1024 * 1024),
    )(*results)
    shape = (1, micro, tokens, width)
    return (acts.reshape(shape), grads.reshape(shape), wgrad[None])


def solution(mesh):
    in_specs = (
        P(None, "dp", None),
        P(None, "dp", None),
        P("section", None, None),
        P("section", None),
    )
    out_specs = (
        P("section", None, "dp", None),
        P("section", None, "dp", None),
        P("section", "dp", None),
    )
    return jax.shard_map(body, mesh=mesh, in_specs=in_specs, out_specs=out_specs, check_vma=False)
```

```python
import jax
import jax.numpy as jnp
from jax import lax
from jax.experimental import pallas as pl
from jax.experimental.pallas import tpu as pltpu
from jax.sharding import PartitionSpec as P

EPS = 1e-05
MESH = pl.DeviceIdType.MESH
BF16, F32 = jnp.bfloat16, jnp.float32

CHUNK = 16
PIECES = 5
GROUP = 64
PAIRED = 2
SINGLES = 2
AHEAD = 3
BLOCKS = ((0, 1), (2, 3, 4))
PADDED = 128


def kernel(
    x_hbm, d_hbm, w_hbm, gain, acts_out, grads_out, wgrad_out,
    w_v, wt_v, xs, ds_in, acts, grads, pre, rinv, acc, slopes, nx, nt, sx, partial,
    to_twin, from_twin, to_across, from_across, to_x, from_x, wgrad,
    w_sem, out_sem, f_send, f_recv, b_send, b_recv, n_send, n_recv, s_send, s_recv,
    t_send, t_recv, y_send, y_recv, o_send, o_recv,
):
    total, width = xs.shape
    count = total // CHUNK
    piece = width // PIECES
    window = sx.shape[1]
    share = wgrad.shape[0]
    per_group = GROUP // CHUNK
    groups = total // GROUP
    deep = 4 * GROUP
    section, dp = lax.axis_index("section"), lax.axis_index("dp")
    sections = lax.axis_size("section")
    x, y, core = dp // 4, (dp // 2) % 2, dp % 2
    first, last = section == 0, section == sections - 1
    early = section >= sections // 2

    def at(x_to, y_to, core_to):
        return (section, x_to * 4 + y_to * 2 + core_to)

    after, before = (section + 1, dp), (section - 1, dp)
    twin, across = at(x, y, 1 - core), at(x, 1 - y, core)
    steps = (1, 3, 2)
    others = [(x + step) % 4 for step in steps]

    def local(source, target, sem):
        return pltpu.make_async_copy(source, target, sem)

    def remote(source, target, send, recv, device):
        return pltpu.make_async_remote_copy(
            src_ref=source, dst_ref=target, send_sem=send, recv_sem=recv, device_id=device, device_id_type=MESH
        )

    def cols(p):
        return slice(p * piece, (p + 1) * piece)

    def rows_of(m, n=1):
        return pl.ds(pl.multiple_of(m * CHUNK, CHUNK), n * CHUNK)

    def slot(m, source, n=1):
        start = (m // per_group) * deep + source * GROUP + (m % per_group) * CHUNK
        return pl.ds(pl.multiple_of(start, CHUNK), n * CHUNK)

    def window_of(owner):
        return pl.ds(pl.multiple_of(owner * window, 128), window)

    def fetch_x(m):
        for p in range(PIECES):
            here = (rows_of(m), cols(p))
            local(x_hbm.at[here], xs.at[here], f_recv.at[m, p]).start()

    def fetch_d(m):
        for p in range(PIECES):
            here = (rows_of(m), cols(p))
            local(d_hbm.at[here], ds_in.at[here], b_recv.at[m, p]).start()

    def fetch_w(p):
        return local(w_hbm.at[cols(p), :], w_v.at[cols(p), :], w_sem.at[p])

    def push_acts(m, p):
        here = (rows_of(m), cols(p))
        return remote(acts.at[here], xs.at[here], f_send.at[m, p], f_recv.at[m, p], after)

    def push_grads(m, p):
        here = (rows_of(m), cols(p))
        return remote(grads.at[here], ds_in.at[here], b_send.at[m, p], b_recv.at[m, p], before)

    def push_normed(m, k):
        here = nx.at[slot(m, x), :]
        return remote(here, here, n_send.at[k, m], n_recv.at[k, m], at(others[k], y, core))

    def push_s(m, k):
        return remote(
            slopes.at[rows_of(m), window_of(others[k])],
            sx.at[slot(m, x), :],
            s_send.at[k, m],
            s_recv.at[k, m],
            at(others[k], y, core),
        )

    def keep_acts(m):
        return local(acts.at[rows_of(m), :], acts_out.at[rows_of(m), :], out_sem.at[0, m])

    def keep_grads(m):
        return local(grads.at[rows_of(m), :], grads_out.at[rows_of(m), :], out_sem.at[1, m])

    @pl.when(first)
    def _():
        fetch_x(0)

    for p in range(PIECES):
        fetch_w(p).start()

    @pl.when(first)
    def _():
        fetch_x(1)

    @pl.when(last)
    def _():
        @pl.loop(0, count)
        def _(m):
            fetch_d(m)

    barrier = pltpu.get_barrier_semaphore()
    for device in [twin, across] + [at(other, y, core) for other in others]:
        pl.semaphore_signal(barrier, inc=1, device_id=device, device_id_type=MESH)

    @pl.when(section > 0)
    def _():
        pl.semaphore_signal(barrier, inc=1, device_id=before, device_id_type=MESH)

    @pl.when(section < sections - 1)
    def _():
        pl.semaphore_signal(barrier, inc=1, device_id=after, device_id_type=MESH)

    pl.semaphore_wait(barrier, 5 + (section > 0).astype(jnp.int32) + (section < sections - 1).astype(jnp.int32))

    def turn_weight():
        tile = 256

        @pl.loop(0, width // tile)
        def _(i):
            i = pl.ds(pl.multiple_of(i * tile, tile), tile)
            for j in range(0, width, tile):
                wt_v[j : j + tile, i] = w_v[i, j : j + tile].T

    def turn_normed():
        for k in range(3):

            @pl.loop(0, count)
            def _(m):
                push_normed(m, k).wait_recv()

        tile = 256

        @pl.loop(0, width // tile)
        def _(i):
            i = pl.ds(pl.multiple_of(i * tile, tile), tile)
            for g in range(groups):
                g = slice(g * deep, (g + 1) * deep)
                nt[i, g] = nx[g, i].T

    def await_group(g):
        for k in range(3):
            for i in range(per_group):
                push_s(g * per_group + i, k).wait_recv()

    @pl.when(jnp.logical_not(first))
    def _():
        for p in range(PIECES):
            fetch_w(p).wait()

    @pl.when(early)
    def _():
        turn_weight()

    def add_product(lhs, rhs, p, taken):
        tile = 512
        if taken > CHUNK:
            lhs = jnp.concatenate([lhs, jnp.zeros((PADDED - taken, piece), BF16)], 0)
        for j in range(0, width, tile):
            term = jnp.dot(lhs, rhs[cols(p), j : j + tile], preferred_element_type=F32)[:taken]
            if p == 0:
                acc[:taken, j : j + tile] = term
            else:
                acc[:taken, j : j + tile] += term

    def lane_sum(values):
        out = values[:, :128]
        for j in range(128, values.shape[1], 128):
            out = out + values[:, j : j + 128]
        return out

    def forward(m, n, cold=False):
        rows = rows_of(m, n)
        taken = n * CHUNK
        squares = None
        for p in range(PIECES):

            for i in range(n):
                here = xs.at[rows_of(m + i), cols(p)]
                local(here, here, f_recv.at[m + i, p]).wait()
            if cold:
                fetch_w(p).wait()
            xf = xs[rows, cols(p)].astype(F32)
            term = lane_sum(xf * xf)
            squares = term if squares is None else squares + term
            add_product((xf * gain[:, cols(p)]).astype(BF16), w_v, p, taken)
        r = lax.rsqrt(jnp.sum(squares, -1, keepdims=True) * (1.0 / width) + EPS)
        for block in BLOCKS:
            for p in block:
                a = acc[:taken, cols(p)] * r
                pre[rows, cols(p)] = a
                acts[rows, cols(p)] = (xs[rows, cols(p)].astype(F32) + a * jax.nn.sigmoid(a)).astype(BF16)

            @pl.when(section < sections - 1)
            def _():
                for i in range(n):
                    for p in block:
                        push_acts(m + i, p).start()

        if n == 1:

            @pl.when(jnp.logical_and(first, m + 2 < count))
            def _():
                fetch_x(m + 2)

        rinv[rows, :] = jnp.broadcast_to(r, (taken, 128))
        for p in range(PIECES):
            nx[slot(m, x, n), cols(p)] = (xs[rows, cols(p)].astype(F32) * r * gain[:, cols(p)]).astype(BF16)
        for i in range(n):
            keep_acts(m + i).start()
            for k in range(3):
                push_normed(m + i, k).start()

    def backward(m, n):
        rows = rows_of(m, n)
        taken = n * CHUNK
        dots = None
        for p in range(PIECES):
            a = pre[rows, cols(p)]
            sig = jax.nn.sigmoid(a)
            slope = sig * (1.0 + a * (1.0 - sig))

            for i in range(n):
                here = ds_in.at[rows_of(m + i), cols(p)]
                local(here, here, b_recv.at[m + i, p]).wait()
            s = (ds_in[rows, cols(p)].astype(F32) * slope).astype(BF16)
            slopes[rows, cols(p)] = s
            term = lane_sum(s.astype(F32) * a)
            dots = term if dots is None else dots + term
            add_product(s, wt_v, p, taken)

        def share_s():
            for i in range(n):
                for k in range(3):
                    push_s(m + i, k).start()

        r = rinv[rows, :1]
        scale = r * r * (jnp.sum(dots, -1, keepdims=True) * (1.0 / width))
        for block in BLOCKS:
            for p in block:
                out = (
                    ds_in[rows, cols(p)].astype(F32)
                    + r * (gain[:, cols(p)] * acc[:taken, cols(p)])
                    - xs[rows, cols(p)].astype(F32) * scale
                )
                grads[rows, cols(p)] = out.astype(BF16)

            @pl.when(section > 0)
            def _():
                for i in range(n):
                    for p in block:
                        push_grads(m + i, p).start()

        share_s()
        sx[slot(m, x, n), :] = slopes[rows, window_of(x)]
        for i in range(n):
            keep_grads(m + i).start()

    behind = sections - 1 - section
    paired = behind < PAIRED
    pairs = (count - 2 * SINGLES) // 2
    lag = jnp.where(paired, AHEAD * behind, count)

    def visit(step, paired, work, skip):
        inside = jnp.logical_and(step >= SINGLES, step < SINGLES + pairs)
        two = jnp.logical_and(paired, inside)
        start = jnp.where(step < SINGLES, step, jnp.where(inside, 2 * step - SINGLES, step + pairs))
        start = jnp.where(paired, start, step)
        active = jnp.logical_and(step >= skip, step < jnp.where(paired, pairs + 2 * SINGLES, count))

        @pl.when(jnp.logical_and(active, two))
        def _():
            work(start, 2)

        @pl.when(jnp.logical_and(active, jnp.logical_not(two)))
        def _():
            work(start, 1)

    @pl.when(first)
    def _():
        forward(0, 1, cold=True)

    @pl.loop(0, 2 * count)
    def _(i):
        visit(i, paired, forward, first.astype(jnp.int32))

        @pl.when(jnp.logical_and(i == count - 1, jnp.logical_not(early)))
        def _():
            turn_weight()
            turn_normed()

        visit(i - lag, paired, backward, 0)

    @pl.when(early)
    def _():
        turn_normed()

    def owner(k):
        step = jnp.where(k == 0, 2, jnp.where(k == 1, 1, jnp.where(k == 2, 3, 0)))
        return (x + step) % 4

    def product(k, y_to, core_to, tokens):
        start = owner(k) * (4 * share) + (y_to * 2 + core_to) * share
        rows = pl.ds(pl.multiple_of(start, 32), share)
        return jnp.dot(nt[rows, tokens], sx[tokens, :], preferred_element_type=F32)

    known, tail = slice(0, (groups - 1) * deep), slice((groups - 1) * deep, groups * deep)
    for g in range(groups - 1):
        await_group(g)

    @pl.loop(0, 4)
    def _(k):
        partial[0, k] = product(k, 1 - y, 1 - core, known)
        partial[1, k] = product(k, 1 - y, core, known)

    await_group(groups - 1)

    def push_twin(half, k):
        return remote(to_twin.at[half, k], from_twin.at[half, k], t_send.at[half, k], t_recv.at[half, k], twin)

    def push_across(k):
        return remote(to_across.at[k], from_across.at[k], y_send.at[k], y_recv.at[k], across)

    def push_owner(k):
        return remote(to_x.at[k], from_x.at[k], o_send.at[k], o_recv.at[k], at(owner(k), y, core))

    def keep_wgrad(source):
        return local(wgrad.at[:, window_of(source)], wgrad_out.at[:, window_of(source)], out_sem.at[2, source])

    norm = float(4096) ** (-0.5)

    @pl.loop(0, 4)
    def _(k):
        to_twin[0, k] = (partial[0, k] + product(k, 1 - y, 1 - core, tail)).astype(BF16)
        push_twin(0, k).start()

    @pl.loop(0, 4)
    def _(k):
        value = partial[1, k] + product(k, 1 - y, core, tail)
        push_twin(0, k).wait_recv()
        to_across[k] = (value + from_twin[0, k].astype(F32)).astype(BF16)
        push_across(k).start()

    @pl.loop(0, 4)
    def _(k):
        to_twin[1, k] = product(k, y, 1 - core, slice(None)).astype(BF16)
        push_twin(1, k).start()

    @pl.loop(0, 4)
    def _(k):
        value = product(k, y, core, slice(None))
        push_twin(1, k).wait_recv()
        partial[0, k] = value + from_twin[1, k].astype(F32)

    @pl.loop(0, 3)
    def _(k):
        push_across(k).wait_recv()
        to_x[k] = (partial[0, k] + from_across[k].astype(F32)).astype(BF16)
        push_owner(k).start()

    push_across(3).wait_recv()
    wgrad[:, window_of(x)] = norm * (partial[0, 3] + from_across[3].astype(F32))
    keep_wgrad(x).start()
    for k, step in enumerate((2, 3, 1)):
        source = (x + step) % 4
        push_owner(k).wait_recv()
        wgrad[:, window_of(source)] = norm * from_x[k].astype(F32)
        keep_wgrad(source).start()

    @pl.loop(0, 4)
    def _(k):
        push_twin(0, k).wait_send()
        push_twin(1, k).wait_send()
        push_across(k).wait_send()

    for k in range(3):
        push_owner(k).wait_send()

    @pl.loop(0, count)
    def _(m):
        for k in range(3):
            push_normed(m, k).wait_send()
            push_s(m, k).wait_send()
        keep_acts(m).wait()
        keep_grads(m).wait()
        for p in range(PIECES):

            @pl.when(section < sections - 1)
            def _():
                push_acts(m, p).wait_send()

            @pl.when(section > 0)
            def _():
                push_grads(m, p).wait_send()

    for k in range(4):
        keep_wgrad(k).wait()


def place(acts_in, grads_in, wgrad_in, acts, grads, wgrad, held, held_wide, in_sems, out_sems):
    parts = 4
    loads, stores = [], []
    arrays = ((acts_in, held.at[0], acts), (grads_in, held.at[1], grads), (wgrad_in, held_wide, wgrad))
    for k, (source, middle, target) in enumerate(arrays):
        step = source.shape[0] // parts
        for i in range(parts):
            rows = slice(i * step, (i + 1) * step)
            loads.append(pltpu.make_async_copy(source.at[rows, :], middle.at[rows, :], in_sems.at[k, i]))
            stores.append(pltpu.make_async_copy(middle.at[rows, :], target.at[rows, :], out_sems.at[k, i]))
    for load in loads:
        load.start()
    for load, store in zip(loads, stores):
        load.wait()
        store.start()
    for store in stores:
        store.wait()


def body(inputs, cotangent, weight, gain):
    micro, tokens, width = inputs.shape
    total = micro * tokens
    share = width // lax.axis_size("dp")
    window = 4 * share
    count = total // CHUNK
    vmem, dma = pltpu.VMEM, pltpu.SemaphoreType.DMA
    anywhere = pl.BlockSpec(memory_space=pl.ANY)
    shapes = (
        jax.ShapeDtypeStruct((total, width), BF16),
        jax.ShapeDtypeStruct((total, width), BF16),
        jax.ShapeDtypeStruct((share, width), F32),
    )
    results = pl.pallas_call(
        kernel,
        out_shape=shapes,
        in_specs=[anywhere] * 3 + [pl.BlockSpec(memory_space=vmem)],
        out_specs=[anywhere] * 3,
        scratch_shapes=[
            vmem((width, width), BF16),
            vmem((width, width), BF16),
            vmem((total, width), BF16),
            vmem((total, width), BF16),
            vmem((total, width), BF16),
            vmem((total, width), BF16),
            vmem((total, width), F32),
            vmem((total, 128), F32),
            vmem((2 * CHUNK, width), F32),
            vmem((total, width), BF16),
            vmem((4 * total, width), BF16),
            vmem((width, 4 * total), BF16),
            vmem((4 * total, window), BF16),
            vmem((2, 4, share, window), F32),
            vmem((2, 4, share, window), BF16),
            vmem((2, 4, share, window), BF16),
            vmem((4, share, window), BF16),
            vmem((4, share, window), BF16),
            vmem((3, share, window), BF16),
            vmem((3, share, window), BF16),
            vmem((share, width), F32),
            dma((PIECES,)),
            dma((3, count)),
            dma((count, PIECES)),
            dma((count, PIECES)),
            dma((count, PIECES)),
            dma((count, PIECES)),
            dma((3, count)),
            dma((3, count)),
            dma((3, count)),
            dma((3, count)),
            dma((2, 4)),
            dma((2, 4)),
            dma((4,)),
            dma((4,)),
            dma((3,)),
            dma((3,)),
        ],
        compiler_params=pltpu.CompilerParams(
            collective_id=0, has_side_effects=True, vmem_limit_bytes=62 * 1024 * 1024
        ),
    )(inputs.reshape(total, width), cotangent.reshape(total, width), weight[0], gain)
    acts, grads, wgrad = pl.pallas_call(
        place,
        out_shape=shapes,
        in_specs=[anywhere] * 3,
        out_specs=[anywhere] * 3,
        scratch_shapes=[vmem((2, total, width), BF16), vmem((share, width), F32), dma((3, 4)), dma((3, 4))],
        compiler_params=pltpu.CompilerParams(vmem_limit_bytes=62 * 1024 * 1024),
    )(*results)
    shape = (1, micro, tokens, width)
    return (acts.reshape(shape), grads.reshape(shape), wgrad[None])


def solution(mesh):
    in_specs = (
        P(None, "dp", None),
        P(None, "dp", None),
        P("section", None, None),
        P("section", None),
    )
    out_specs = (
        P("section", None, "dp", None),
        P("section", None, "dp", None),
        P("section", "dp", None),
    )
    return jax.shard_map(body, mesh=mesh, in_specs=in_specs, out_specs=out_specs, check_vma=False)
```

```python
import jax
import jax.numpy as jnp
from jax import lax
from jax.experimental import pallas as pl
from jax.experimental.pallas import tpu as pltpu
from jax.sharding import PartitionSpec as P

EPS = 1e-05
MESH = pl.DeviceIdType.MESH
BF16, F32 = jnp.bfloat16, jnp.float32

CHUNK = 16
PIECES = 5
GROUP = 64
PAIRED = 2
SINGLES = 2
AHEAD = 3
BLOCKS = ((0, 1), (2, 3, 4))
PADDED = 128


def kernel(
    x_hbm, d_hbm, w_hbm, gain, acts_out, grads_out, wgrad_out,
    w_v, wt_v, xs, ds_in, acts, grads, pre, rinv, acc, slopes, nx, nt, sx, partial,
    to_twin, from_twin, to_across, from_across, to_x, from_x, wgrad,
    w_sem, out_sem, home_sem, f_send, f_recv, b_send, b_recv, n_send, n_recv, s_send, s_recv,
    t_send, t_recv, y_send, y_recv, o_send, o_recv,
):
    total, width = xs.shape
    count = total // CHUNK
    piece = width // PIECES
    window = sx.shape[1]
    share = wgrad.shape[0]
    per_group = GROUP // CHUNK
    groups = total // GROUP
    deep = 4 * GROUP
    section, dp = lax.axis_index("section"), lax.axis_index("dp")
    sections = lax.axis_size("section")
    x, y, core = dp // 4, (dp // 2) % 2, dp % 2
    first, last = section == 0, section == sections - 1
    early = section >= sections // 2

    def at(x_to, y_to, core_to):
        return (section, x_to * 4 + y_to * 2 + core_to)

    twin, across = at(x, y, 1 - core), at(x, 1 - y, core)
    odd = section % 2 == 1
    after, before = (section + 1, across[1]), (section - 1, across[1])
    steps = (1, 3, 2)
    others = [(x + step) % 4 for step in steps]

    def local(source, target, sem):
        return pltpu.make_async_copy(source, target, sem)

    def remote(source, target, send, recv, device):
        return pltpu.make_async_remote_copy(
            src_ref=source, dst_ref=target, send_sem=send, recv_sem=recv, device_id=device, device_id_type=MESH
        )

    def cols(p):
        return slice(p * piece, (p + 1) * piece)

    def rows_of(m, n=1):
        return pl.ds(pl.multiple_of(m * CHUNK, CHUNK), n * CHUNK)

    def slot(m, source, n=1):
        start = (m // per_group) * deep + source * GROUP + (m % per_group) * CHUNK
        return pl.ds(pl.multiple_of(start, CHUNK), n * CHUNK)

    def window_of(owner):
        return pl.ds(pl.multiple_of(owner * window, 128), window)

    def fetch_x(m):
        for p in range(PIECES):
            here = (rows_of(m), cols(p))
            local(x_hbm.at[here], xs.at[here], f_recv.at[m, p]).start()

    def fetch_d(m):
        for p in range(PIECES):
            here = (rows_of(m), cols(p))
            yield remote(d_hbm.at[here], ds_in.at[here], f_send.at[m, p], b_recv.at[m, p], across)

    def fetch_w(p):
        return local(w_hbm.at[cols(p), :], w_v.at[cols(p), :], w_sem.at[p])

    def push_acts(m, p):
        here = (rows_of(m), cols(p))
        return remote(acts.at[here], xs.at[here], f_send.at[m, p], f_recv.at[m, p], after)

    def push_grads(m, p):
        here = (rows_of(m), cols(p))
        return remote(grads.at[here], ds_in.at[here], b_send.at[m, p], b_recv.at[m, p], before)

    def push_normed(m, k):
        here = nx.at[slot(m, x), :]
        return remote(here, here, n_send.at[k, m], n_recv.at[k, m], at(others[k], y, core))

    def push_s(m, k):
        return remote(
            slopes.at[rows_of(m), window_of(others[k])],
            sx.at[slot(m, x), :],
            s_send.at[k, m],
            s_recv.at[k, m],
            at(others[k], y, core),
        )

    def keep(k, m):
        source, target = ((acts, acts_out), (grads, grads_out))[k]
        return local(source.at[rows_of(m), :], target.at[rows_of(m), :], out_sem.at[k, m])

    def home(k, m):
        source, target = ((acts, acts_out), (grads, grads_out))[k]
        return remote(
            source.at[rows_of(m), :], target.at[rows_of(m), :], out_sem.at[k, m], home_sem.at[k, m], across
        )

    def leave(k, m):
        @pl.when(odd)
        def _():
            home(k, m).start()

        @pl.when(jnp.logical_not(odd))
        def _():
            keep(k, m).start()

    @pl.when(first)
    def _():
        fetch_x(0)

    for p in range(PIECES):
        fetch_w(p).start()

    @pl.when(first)
    def _():
        fetch_x(1)

    barrier = pltpu.get_barrier_semaphore()
    for device in [twin, across] + [at(other, y, core) for other in others]:
        pl.semaphore_signal(barrier, inc=1, device_id=device, device_id_type=MESH)

    @pl.when(section > 0)
    def _():
        pl.semaphore_signal(barrier, inc=1, device_id=before, device_id_type=MESH)

    @pl.when(section < sections - 1)
    def _():
        pl.semaphore_signal(barrier, inc=1, device_id=after, device_id_type=MESH)

    pl.semaphore_wait(barrier, 5 + (section > 0).astype(jnp.int32) + (section < sections - 1).astype(jnp.int32))

    @pl.when(last)
    def _():
        @pl.loop(0, count)
        def _(m):
            for copy in fetch_d(m):
                copy.start()

    def turn_weight():
        tile = 256

        @pl.loop(0, width // tile)
        def _(i):
            i = pl.ds(pl.multiple_of(i * tile, tile), tile)
            for j in range(0, width, tile):
                wt_v[j : j + tile, i] = w_v[i, j : j + tile].T

    def turn_normed():
        for k in range(3):

            @pl.loop(0, count)
            def _(m):
                push_normed(m, k).wait_recv()

        tile = 256

        @pl.loop(0, width // tile)
        def _(i):
            i = pl.ds(pl.multiple_of(i * tile, tile), tile)
            for g in range(groups):
                g = slice(g * deep, (g + 1) * deep)
                nt[i, g] = nx[g, i].T

    def await_group(g):
        for k in range(3):
            for i in range(per_group):
                push_s(g * per_group + i, k).wait_recv()

    @pl.when(jnp.logical_not(first))
    def _():
        for p in range(PIECES):
            fetch_w(p).wait()

    @pl.when(early)
    def _():
        turn_weight()

    def add_product(lhs, rhs, p, taken):
        tile = 512
        if taken > CHUNK:
            lhs = jnp.concatenate([lhs, jnp.zeros((PADDED - taken, piece), BF16)], 0)
        for j in range(0, width, tile):
            term = jnp.dot(lhs, rhs[cols(p), j : j + tile], preferred_element_type=F32)[:taken]
            if p == 0:
                acc[:taken, j : j + tile] = term
            else:
                acc[:taken, j : j + tile] += term

    def lane_sum(values):
        out = values[:, :128]
        for j in range(128, values.shape[1], 128):
            out = out + values[:, j : j + 128]
        return out

    def forward(m, n, cold=False):
        rows = rows_of(m, n)
        taken = n * CHUNK
        squares = None
        for p in range(PIECES):

            for i in range(n):
                here = xs.at[rows_of(m + i), cols(p)]
                local(here, here, f_recv.at[m + i, p]).wait()
            if cold:
                fetch_w(p).wait()
            xf = xs[rows, cols(p)].astype(F32)
            term = lane_sum(xf * xf)
            squares = term if squares is None else squares + term
            add_product((xf * gain[:, cols(p)]).astype(BF16), w_v, p, taken)
        r = lax.rsqrt(jnp.sum(squares, -1, keepdims=True) * (1.0 / width) + EPS)
        for block in BLOCKS:
            for p in block:
                a = acc[:taken, cols(p)] * r
                pre[rows, cols(p)] = a
                acts[rows, cols(p)] = (xs[rows, cols(p)].astype(F32) + a * jax.nn.sigmoid(a)).astype(BF16)

            @pl.when(section < sections - 1)
            def _():
                for i in range(n):
                    for p in block:
                        push_acts(m + i, p).start()

        if n == 1:

            @pl.when(jnp.logical_and(first, m + 2 < count))
            def _():
                fetch_x(m + 2)

        rinv[rows, :] = jnp.broadcast_to(r, (taken, 128))
        for p in range(PIECES):
            nx[slot(m, x, n), cols(p)] = (xs[rows, cols(p)].astype(F32) * r * gain[:, cols(p)]).astype(BF16)
        for i in range(n):
            leave(0, m + i)
            for k in range(3):
                push_normed(m + i, k).start()

    def backward(m, n, eager=False):
        rows = rows_of(m, n)
        taken = n * CHUNK
        dots = None
        for p in range(PIECES):
            a = pre[rows, cols(p)]
            sig = jax.nn.sigmoid(a)
            slope = sig * (1.0 + a * (1.0 - sig))

            for i in range(n):
                here = ds_in.at[rows_of(m + i), cols(p)]
                local(here, here, b_recv.at[m + i, p]).wait()
            s = (ds_in[rows, cols(p)].astype(F32) * slope).astype(BF16)
            slopes[rows, cols(p)] = s
            term = lane_sum(s.astype(F32) * a)
            dots = term if dots is None else dots + term
            if not eager:
                add_product(s, wt_v, p, taken)

        def share_s():
            for i in range(n):
                for k in range(3):
                    push_s(m + i, k).start()

        if eager:
            share_s()
            for p in range(PIECES):
                add_product(slopes[rows, cols(p)], wt_v, p, taken)
        r = rinv[rows, :1]
        scale = r * r * (jnp.sum(dots, -1, keepdims=True) * (1.0 / width))
        for block in BLOCKS:
            for p in block:
                out = (
                    ds_in[rows, cols(p)].astype(F32)
                    + r * (gain[:, cols(p)] * acc[:taken, cols(p)])
                    - xs[rows, cols(p)].astype(F32) * scale
                )
                grads[rows, cols(p)] = out.astype(BF16)

            if not eager:

                @pl.when(section > 0)
                def _():
                    for i in range(n):
                        for p in block:
                            push_grads(m + i, p).start()

        if not eager:
            share_s()
        sx[slot(m, x, n), :] = slopes[rows, window_of(x)]
        for i in range(n):
            leave(1, m + i)

    behind = sections - 1 - section
    paired = behind < PAIRED
    pairs = (count - 2 * SINGLES) // 2
    lag = jnp.where(paired, AHEAD * behind, count)

    def visit(step, work, skip, spare):
        inside = jnp.logical_and(step >= SINGLES, step < SINGLES + pairs)
        two = jnp.logical_and(paired, inside)
        start = jnp.where(step < SINGLES, step, jnp.where(inside, 2 * step - SINGLES, step + pairs))
        start = jnp.where(paired, start, step)
        active = jnp.logical_and(step >= skip, step < jnp.where(paired, pairs + 2 * SINGLES, count) - spare)

        @pl.when(jnp.logical_and(active, two))
        def _():
            work(start, 2)

        @pl.when(jnp.logical_and(active, jnp.logical_not(two)))
        def _():
            work(start, 1)

    @pl.when(first)
    def _():
        forward(0, 1, cold=True)

    @pl.loop(0, 2 * count)
    def _(i):
        visit(i, forward, first.astype(jnp.int32), 0)

        @pl.when(jnp.logical_and(i == count - 1, jnp.logical_not(early)))
        def _():
            turn_weight()
            turn_normed()

        visit(i - lag, backward, 0, first.astype(jnp.int32))

    @pl.when(first)
    def _():
        backward(count - 1, 1, eager=True)

    @pl.when(early)
    def _():
        turn_normed()

    def owner(k):
        step = jnp.where(k == 0, 2, jnp.where(k == 1, 1, jnp.where(k == 2, 3, 0)))
        return (x + step) % 4

    def product(k, y_to, core_to, tokens):
        start = owner(k) * (4 * share) + (y_to * 2 + core_to) * share
        rows = pl.ds(pl.multiple_of(start, 32), share)
        return jnp.dot(nt[rows, tokens], sx[tokens, :], preferred_element_type=F32)

    known, tail = slice(0, (groups - 1) * deep), slice((groups - 1) * deep, groups * deep)
    for g in range(groups - 1):
        await_group(g)

    @pl.loop(0, 4)
    def _(k):
        partial[0, k] = product(k, 1 - y, 1 - core, known)
        partial[1, k] = product(k, 1 - y, core, known)

    await_group(groups - 1)

    def push_twin(half, k):
        return remote(to_twin.at[half, k], from_twin.at[half, k], t_send.at[half, k], t_recv.at[half, k], twin)

    def push_across(k):
        return remote(to_across.at[k], from_across.at[k], y_send.at[k], y_recv.at[k], across)

    def push_owner(k):
        return remote(to_x.at[k], from_x.at[k], o_send.at[k], o_recv.at[k], at(owner(k), y, core))

    def keep_wgrad(source):
        return local(wgrad.at[:, window_of(source)], wgrad_out.at[:, window_of(source)], out_sem.at[2, source])

    norm = float(4096) ** (-0.5)

    @pl.loop(0, 4)
    def _(k):
        to_twin[0, k] = (partial[0, k] + product(k, 1 - y, 1 - core, tail)).astype(BF16)
        push_twin(0, k).start()

    @pl.loop(0, 4)
    def _(k):
        value = partial[1, k] + product(k, 1 - y, core, tail)
        push_twin(0, k).wait_recv()
        to_across[k] = (value + from_twin[0, k].astype(F32)).astype(BF16)
        push_across(k).start()

    @pl.loop(0, 4)
    def _(k):
        to_twin[1, k] = product(k, y, 1 - core, slice(None)).astype(BF16)
        push_twin(1, k).start()

    @pl.loop(0, 4)
    def _(k):
        value = product(k, y, core, slice(None))
        push_twin(1, k).wait_recv()
        partial[0, k] = value + from_twin[1, k].astype(F32)

    @pl.loop(0, count)
    def _(m):
        for k in range(3):
            push_normed(m, k).wait_send()
            push_s(m, k).wait_send()
        for k in range(2):

            @pl.when(odd)
            def _():
                home(k, m).wait()

            @pl.when(jnp.logical_not(odd))
            def _():
                keep(k, m).wait()

        @pl.when(last)
        def _():
            for copy in fetch_d(m):
                copy.wait_send()

        for p in range(PIECES):

            @pl.when(section < sections - 1)
            def _():
                push_acts(m, p).wait_send()

            @pl.when(section > 0)
            def _():
                push_grads(m, p).wait_send()

    @pl.loop(0, 3)
    def _(k):
        push_across(k).wait_recv()
        to_x[k] = (partial[0, k] + from_across[k].astype(F32)).astype(BF16)
        push_owner(k).start()

    push_across(3).wait_recv()
    wgrad[:, window_of(x)] = norm * (partial[0, 3] + from_across[3].astype(F32))
    keep_wgrad(x).start()
    for k, step in enumerate((2, 3, 1)):
        source = (x + step) % 4
        push_owner(k).wait_recv()
        wgrad[:, window_of(source)] = norm * from_x[k].astype(F32)
        keep_wgrad(source).start()

    @pl.loop(0, 4)
    def _(k):
        push_twin(0, k).wait_send()
        push_twin(1, k).wait_send()
        push_across(k).wait_send()

    for k in range(3):
        push_owner(k).wait_send()

    for k in range(4):
        keep_wgrad(k).wait()


def place(acts_in, grads_in, wgrad_in, acts, grads, wgrad, held, held_wide, in_sems, out_sems):
    parts = 4
    loads, stores = [], []
    arrays = ((acts_in, held.at[0], acts), (grads_in, held.at[1], grads), (wgrad_in, held_wide, wgrad))
    for k, (source, middle, target) in enumerate(arrays):
        step = source.shape[0] // parts
        for i in range(parts):
            rows = slice(i * step, (i + 1) * step)
            loads.append(pltpu.make_async_copy(source.at[rows, :], middle.at[rows, :], in_sems.at[k, i]))
            stores.append(pltpu.make_async_copy(middle.at[rows, :], target.at[rows, :], out_sems.at[k, i]))
    for load in loads:
        load.start()
    for load, store in zip(loads, stores):
        load.wait()
        store.start()
    for store in stores:
        store.wait()


def body(inputs, cotangent, weight, gain):
    micro, tokens, width = inputs.shape
    total = micro * tokens
    share = width // lax.axis_size("dp")
    window = 4 * share
    count = total // CHUNK
    vmem, dma = pltpu.VMEM, pltpu.SemaphoreType.DMA
    anywhere = pl.BlockSpec(memory_space=pl.ANY)
    shapes = (
        jax.ShapeDtypeStruct((total, width), BF16),
        jax.ShapeDtypeStruct((total, width), BF16),
        jax.ShapeDtypeStruct((share, width), F32),
    )
    results = pl.pallas_call(
        kernel,
        out_shape=shapes,
        in_specs=[anywhere] * 3 + [pl.BlockSpec(memory_space=vmem)],
        out_specs=[anywhere] * 3,
        scratch_shapes=[
            vmem((width, width), BF16),
            vmem((width, width), BF16),
            vmem((total, width), BF16),
            vmem((total, width), BF16),
            vmem((total, width), BF16),
            vmem((total, width), BF16),
            vmem((total, width), F32),
            vmem((total, 128), F32),
            vmem((2 * CHUNK, width), F32),
            vmem((total, width), BF16),
            vmem((4 * total, width), BF16),
            vmem((width, 4 * total), BF16),
            vmem((4 * total, window), BF16),
            vmem((2, 4, share, window), F32),
            vmem((2, 4, share, window), BF16),
            vmem((2, 4, share, window), BF16),
            vmem((4, share, window), BF16),
            vmem((4, share, window), BF16),
            vmem((3, share, window), BF16),
            vmem((3, share, window), BF16),
            vmem((share, width), F32),
            dma((PIECES,)),
            dma((3, count)),
            dma((2, count)),
            dma((count, PIECES)),
            dma((count, PIECES)),
            dma((count, PIECES)),
            dma((count, PIECES)),
            dma((3, count)),
            dma((3, count)),
            dma((3, count)),
            dma((3, count)),
            dma((2, 4)),
            dma((2, 4)),
            dma((4,)),
            dma((4,)),
            dma((3,)),
            dma((3,)),
        ],
        compiler_params=pltpu.CompilerParams(
            collective_id=0, has_side_effects=True, vmem_limit_bytes=62 * 1024 * 1024
        ),
    )(inputs.reshape(total, width), cotangent.reshape(total, width), weight[0], gain)
    acts, grads, wgrad = pl.pallas_call(
        place,
        out_shape=shapes,
        in_specs=[anywhere] * 3,
        out_specs=[anywhere] * 3,
        scratch_shapes=[vmem((2, total, width), BF16), vmem((share, width), F32), dma((3, 4)), dma((3, 4))],
        compiler_params=pltpu.CompilerParams(vmem_limit_bytes=62 * 1024 * 1024),
    )(*results)
    shape = (1, micro, tokens, width)
    return (acts.reshape(shape), grads.reshape(shape), wgrad[None])


def solution(mesh):
    in_specs = (
        P(None, "dp", None),
        P(None, "dp", None),
        P("section", None, None),
        P("section", None),
    )
    out_specs = (
        P("section", None, "dp", None),
        P("section", None, "dp", None),
        P("section", "dp", None),
    )
    return jax.shard_map(body, mesh=mesh, in_specs=in_specs, out_specs=out_specs, check_vma=False)
```

```python
import jax
import jax.numpy as jnp
from jax import lax
from jax.experimental import pallas as pl
from jax.experimental.pallas import tpu as pltpu
from jax.sharding import PartitionSpec as P

EPS = 1e-05
MESH = pl.DeviceIdType.MESH
BF16, F32 = jnp.bfloat16, jnp.float32

CHUNK = 16
EDGES = (0, 256, 768, 1280, 1792, 2304, 2560)
PIECES = len(EDGES) - 1
GROUP = 64
PAIRED = 2
SINGLES = 2
AHEAD = 3
BLOCKS = ((0, 1), (2, 3, 4, 5))
PADDED = 128


def kernel(
    x_hbm, d_hbm, w_hbm, gain, acts_out, grads_out, wgrad_out,
    w_v, wt_v, xs, ds_in, acts, grads, pre, rinv, acc, slopes, nx, nt, sx, partial,
    to_twin, from_twin, to_across, from_across, to_x, from_x, wgrad,
    w_sem, out_sem, home_sem, f_send, f_recv, b_send, b_recv, n_send, n_recv, s_send, s_recv,
    t_send, t_recv, y_send, y_recv, o_send, o_recv,
):
    total, width = xs.shape
    count = total // CHUNK
    window = sx.shape[1]
    share = wgrad.shape[0]
    per_group = GROUP // CHUNK
    groups = total // GROUP
    deep = 4 * GROUP
    section, dp = lax.axis_index("section"), lax.axis_index("dp")
    sections = lax.axis_size("section")
    x, y, core = dp // 4, (dp // 2) % 2, dp % 2
    first, last = section == 0, section == sections - 1
    early = section >= sections // 2

    def at(x_to, y_to, core_to):
        return (section, x_to * 4 + y_to * 2 + core_to)

    twin, across = at(x, y, 1 - core), at(x, 1 - y, core)
    odd = section % 2 == 1
    after, before = (section + 1, across[1]), (section - 1, across[1])
    steps = (1, 3, 2)
    others = [(x + step) % 4 for step in steps]

    def local(source, target, sem):
        return pltpu.make_async_copy(source, target, sem)

    def remote(source, target, send, recv, device):
        return pltpu.make_async_remote_copy(
            src_ref=source, dst_ref=target, send_sem=send, recv_sem=recv, device_id=device, device_id_type=MESH
        )

    def cols(p):
        return slice(EDGES[p], EDGES[p + 1])

    def rows_of(m, n=1):
        return pl.ds(pl.multiple_of(m * CHUNK, CHUNK), n * CHUNK)

    def slot(m, source, n=1):
        start = (m // per_group) * deep + source * GROUP + (m % per_group) * CHUNK
        return pl.ds(pl.multiple_of(start, CHUNK), n * CHUNK)

    def window_of(owner):
        return pl.ds(pl.multiple_of(owner * window, 128), window)

    def fetch_x(m):
        for p in range(PIECES):
            here = (rows_of(m), cols(p))
            local(x_hbm.at[here], xs.at[here], f_recv.at[m, p]).start()

    def fetch_d(m):
        for p in range(PIECES):
            here = (rows_of(m), cols(p))
            yield remote(d_hbm.at[here], ds_in.at[here], f_send.at[m, p], b_recv.at[m, p], across)

    def fetch_w(p):
        return local(w_hbm.at[cols(p), :], w_v.at[cols(p), :], w_sem.at[p])

    def push_acts(m, p):
        here = (rows_of(m), cols(p))
        return remote(acts.at[here], xs.at[here], f_send.at[m, p], f_recv.at[m, p], after)

    def push_grads(m, p):
        here = (rows_of(m), cols(p))
        return remote(grads.at[here], ds_in.at[here], b_send.at[m, p], b_recv.at[m, p], before)

    def push_normed(m, k):
        here = nx.at[slot(m, x), :]
        return remote(here, here, n_send.at[k, m], n_recv.at[k, m], at(others[k], y, core))

    def push_s(m, k):
        return remote(
            slopes.at[rows_of(m), window_of(others[k])],
            sx.at[slot(m, x), :],
            s_send.at[k, m],
            s_recv.at[k, m],
            at(others[k], y, core),
        )

    def keep(k, m):
        source, target = ((acts, acts_out), (grads, grads_out))[k]
        return local(source.at[rows_of(m), :], target.at[rows_of(m), :], out_sem.at[k, m])

    def home(k, m):
        source, target = ((acts, acts_out), (grads, grads_out))[k]
        return remote(
            source.at[rows_of(m), :], target.at[rows_of(m), :], out_sem.at[k, m], home_sem.at[k, m], across
        )

    def leave(k, m):
        @pl.when(odd)
        def _():
            home(k, m).start()

        @pl.when(jnp.logical_not(odd))
        def _():
            keep(k, m).start()

    @pl.when(first)
    def _():
        fetch_x(0)

    for p in range(PIECES):
        fetch_w(p).start()

    @pl.when(first)
    def _():
        fetch_x(1)

    barrier = pltpu.get_barrier_semaphore()
    for device in [twin, across] + [at(other, y, core) for other in others]:
        pl.semaphore_signal(barrier, inc=1, device_id=device, device_id_type=MESH)

    @pl.when(section > 0)
    def _():
        pl.semaphore_signal(barrier, inc=1, device_id=before, device_id_type=MESH)

    @pl.when(section < sections - 1)
    def _():
        pl.semaphore_signal(barrier, inc=1, device_id=after, device_id_type=MESH)

    pl.semaphore_wait(barrier, 5 + (section > 0).astype(jnp.int32) + (section < sections - 1).astype(jnp.int32))

    @pl.when(last)
    def _():
        @pl.loop(0, count)
        def _(m):
            for copy in fetch_d(m):
                copy.start()

    def turn_weight():
        tile = 256

        @pl.loop(0, width // tile)
        def _(i):
            i = pl.ds(pl.multiple_of(i * tile, tile), tile)
            for j in range(0, width, tile):
                wt_v[j : j + tile, i] = w_v[i, j : j + tile].T

    def turn_normed():
        for k in range(3):

            @pl.loop(0, count)
            def _(m):
                push_normed(m, k).wait_recv()

        tile = 256

        @pl.loop(0, width // tile)
        def _(i):
            i = pl.ds(pl.multiple_of(i * tile, tile), tile)
            for g in range(groups):
                g = slice(g * deep, (g + 1) * deep)
                nt[i, g] = nx[g, i].T

    def await_group(g):
        for k in range(3):
            for i in range(per_group):
                push_s(g * per_group + i, k).wait_recv()

    @pl.when(jnp.logical_not(first))
    def _():
        for p in range(PIECES):
            fetch_w(p).wait()

    @pl.when(early)
    def _():
        turn_weight()

    def add_product(lhs, rhs, p, taken):
        tile = 512
        if taken > CHUNK:
            lhs = jnp.concatenate([lhs, jnp.zeros((PADDED - taken, lhs.shape[1]), BF16)], 0)
        for j in range(0, width, tile):
            term = jnp.dot(lhs, rhs[cols(p), j : j + tile], preferred_element_type=F32)[:taken]
            if p == 0:
                acc[:taken, j : j + tile] = term
            else:
                acc[:taken, j : j + tile] += term

    def lane_sum(values):
        out = values[:, :128]
        for j in range(128, values.shape[1], 128):
            out = out + values[:, j : j + 128]
        return out

    def forward(m, n, cold=False):
        rows = rows_of(m, n)
        taken = n * CHUNK
        squares = None
        for p in range(PIECES):

            for i in range(n):
                here = xs.at[rows_of(m + i), cols(p)]
                local(here, here, f_recv.at[m + i, p]).wait()
            if cold:
                fetch_w(p).wait()
            xf = xs[rows, cols(p)].astype(F32)
            term = lane_sum(xf * xf)
            squares = term if squares is None else squares + term
            add_product((xf * gain[:, cols(p)]).astype(BF16), w_v, p, taken)
        r = lax.rsqrt(jnp.sum(squares, -1, keepdims=True) * (1.0 / width) + EPS)
        for block in BLOCKS:
            for p in block:
                a = acc[:taken, cols(p)] * r
                pre[rows, cols(p)] = a
                acts[rows, cols(p)] = (xs[rows, cols(p)].astype(F32) + a * jax.nn.sigmoid(a)).astype(BF16)

            @pl.when(section < sections - 1)
            def _():
                for i in range(n):
                    for p in block:
                        push_acts(m + i, p).start()

        if n == 1:

            @pl.when(jnp.logical_and(first, m + 2 < count))
            def _():
                fetch_x(m + 2)

        rinv[rows, :] = jnp.broadcast_to(r, (taken, 128))
        for p in range(PIECES):
            nx[slot(m, x, n), cols(p)] = (xs[rows, cols(p)].astype(F32) * r * gain[:, cols(p)]).astype(BF16)
        for i in range(n):
            leave(0, m + i)
            for k in range(3):
                push_normed(m + i, k).start()

    def backward(m, n, eager=False):
        rows = rows_of(m, n)
        taken = n * CHUNK
        dots = None
        for p in range(PIECES):
            a = pre[rows, cols(p)]
            sig = jax.nn.sigmoid(a)
            slope = sig * (1.0 + a * (1.0 - sig))

            for i in range(n):
                here = ds_in.at[rows_of(m + i), cols(p)]
                local(here, here, b_recv.at[m + i, p]).wait()
            s = (ds_in[rows, cols(p)].astype(F32) * slope).astype(BF16)
            slopes[rows, cols(p)] = s
            term = lane_sum(s.astype(F32) * a)
            dots = term if dots is None else dots + term
            if not eager:
                add_product(s, wt_v, p, taken)

        def share_s():
            for i in range(n):
                for k in range(3):
                    push_s(m + i, k).start()

        if eager:
            share_s()
            for p in range(PIECES):
                add_product(slopes[rows, cols(p)], wt_v, p, taken)
        r = rinv[rows, :1]
        scale = r * r * (jnp.sum(dots, -1, keepdims=True) * (1.0 / width))
        for block in BLOCKS:
            for p in block:
                out = (
                    ds_in[rows, cols(p)].astype(F32)
                    + r * (gain[:, cols(p)] * acc[:taken, cols(p)])
                    - xs[rows, cols(p)].astype(F32) * scale
                )
                grads[rows, cols(p)] = out.astype(BF16)

            if not eager:

                @pl.when(section > 0)
                def _():
                    for i in range(n):
                        for p in block:
                            push_grads(m + i, p).start()

        if not eager:
            share_s()
        sx[slot(m, x, n), :] = slopes[rows, window_of(x)]
        for i in range(n):
            leave(1, m + i)

    behind = sections - 1 - section
    paired = behind < PAIRED
    pairs = (count - 2 * SINGLES) // 2
    lag = jnp.where(paired, AHEAD * behind, count)

    def visit(step, work, skip, spare):
        inside = jnp.logical_and(step >= SINGLES, step < SINGLES + pairs)
        two = jnp.logical_and(paired, inside)
        start = jnp.where(step < SINGLES, step, jnp.where(inside, 2 * step - SINGLES, step + pairs))
        start = jnp.where(paired, start, step)
        active = jnp.logical_and(step >= skip, step < jnp.where(paired, pairs + 2 * SINGLES, count) - spare)

        @pl.when(jnp.logical_and(active, two))
        def _():
            work(start, 2)

        @pl.when(jnp.logical_and(active, jnp.logical_not(two)))
        def _():
            work(start, 1)

    @pl.when(first)
    def _():
        forward(0, 1, cold=True)

    @pl.loop(0, 2 * count)
    def _(i):
        visit(i, forward, first.astype(jnp.int32), 0)

        @pl.when(jnp.logical_and(i == count - 1, jnp.logical_not(early)))
        def _():
            turn_weight()
            turn_normed()

        visit(i - lag, backward, 0, first.astype(jnp.int32))

    @pl.when(first)
    def _():
        backward(count - 1, 1, eager=True)

    @pl.when(early)
    def _():
        turn_normed()

    def owner(k):
        step = jnp.where(k == 0, 2, jnp.where(k == 1, 1, jnp.where(k == 2, 3, 0)))
        return (x + step) % 4

    def product(k, y_to, core_to, tokens):
        start = owner(k) * (4 * share) + (y_to * 2 + core_to) * share
        rows = pl.ds(pl.multiple_of(start, 32), share)
        return jnp.dot(nt[rows, tokens], sx[tokens, :], preferred_element_type=F32)

    known, tail = slice(0, (groups - 1) * deep), slice((groups - 1) * deep, groups * deep)
    for g in range(groups - 1):
        await_group(g)

    @pl.loop(0, 4)
    def _(k):
        partial[0, k] = product(k, 1 - y, 1 - core, known)
        partial[1, k] = product(k, 1 - y, core, known)

    await_group(groups - 1)

    def push_twin(half, k):
        return remote(to_twin.at[half, k], from_twin.at[half, k], t_send.at[half, k], t_recv.at[half, k], twin)

    half = share // 2

    def half_of(h):
        return pl.ds(pl.multiple_of(h * half, 16), half)

    def push_across(k, h):
        here = (k, half_of(h))
        return remote(to_across.at[here], from_across.at[here], y_send.at[k, h], y_recv.at[k, h], across)

    def push_owner(k, h):
        here = (k, half_of(h))
        return remote(to_x.at[here], from_x.at[here], o_send.at[k, h], o_recv.at[k, h], at(owner(k), y, core))

    def keep_wgrad(source):
        return local(wgrad.at[:, window_of(source)], wgrad_out.at[:, window_of(source)], out_sem.at[2, source])

    norm = float(4096) ** (-0.5)

    @pl.loop(0, 4)
    def _(k):
        to_twin[0, k] = (partial[0, k] + product(k, 1 - y, 1 - core, tail)).astype(BF16)
        push_twin(0, k).start()

    @pl.loop(0, 4)
    def _(k):
        value = partial[1, k] + product(k, 1 - y, core, tail)
        push_twin(0, k).wait_recv()
        to_across[k] = (value + from_twin[0, k].astype(F32)).astype(BF16)
        for h in range(2):
            push_across(k, h).start()

    @pl.loop(0, 4)
    def _(k):
        to_twin[1, k] = product(k, y, 1 - core, slice(None)).astype(BF16)
        push_twin(1, k).start()

    @pl.loop(0, 4)
    def _(k):
        value = product(k, y, core, slice(None))
        push_twin(1, k).wait_recv()
        partial[0, k] = value + from_twin[1, k].astype(F32)

    @pl.loop(0, count)
    def _(m):
        for k in range(3):
            push_normed(m, k).wait_send()
            push_s(m, k).wait_send()
        for k in range(2):

            @pl.when(odd)
            def _():
                home(k, m).wait()

            @pl.when(jnp.logical_not(odd))
            def _():
                keep(k, m).wait()

        @pl.when(last)
        def _():
            for copy in fetch_d(m):
                copy.wait_send()

        for p in range(PIECES):

            @pl.when(section < sections - 1)
            def _():
                push_acts(m, p).wait_send()

            @pl.when(section > 0)
            def _():
                push_grads(m, p).wait_send()

    @pl.loop(0, 3)
    def _(k):
        for h in range(2):
            push_across(k, h).wait_recv()
            to_x[k, half_of(h)] = (partial[0, k, half_of(h)] + from_across[k, half_of(h)].astype(F32)).astype(BF16)
            push_owner(k, h).start()

    for h in range(2):
        push_across(3, h).wait_recv()
    wgrad[:, window_of(x)] = norm * (partial[0, 3] + from_across[3].astype(F32))
    keep_wgrad(x).start()
    for k, step in enumerate((2, 3, 1)):
        source = (x + step) % 4
        for h in range(2):
            push_owner(k, h).wait_recv()
        wgrad[:, window_of(source)] = norm * from_x[k].astype(F32)
        keep_wgrad(source).start()

    @pl.loop(0, 4)
    def _(k):
        push_twin(0, k).wait_send()
        push_twin(1, k).wait_send()
        for h in range(2):
            push_across(k, h).wait_send()

    for k in range(3):
        for h in range(2):
            push_owner(k, h).wait_send()

    for k in range(4):
        keep_wgrad(k).wait()


def place(acts_in, grads_in, wgrad_in, acts, grads, wgrad, held, held_wide, in_sems, out_sems):
    parts = 4
    loads, stores = [], []
    arrays = ((acts_in, held.at[0], acts), (grads_in, held.at[1], grads), (wgrad_in, held_wide, wgrad))
    for k, (source, middle, target) in enumerate(arrays):
        step = source.shape[0] // parts
        for i in range(parts):
            rows = slice(i * step, (i + 1) * step)
            loads.append(pltpu.make_async_copy(source.at[rows, :], middle.at[rows, :], in_sems.at[k, i]))
            stores.append(pltpu.make_async_copy(middle.at[rows, :], target.at[rows, :], out_sems.at[k, i]))
    for load in loads:
        load.start()
    for load, store in zip(loads, stores):
        load.wait()
        store.start()
    for store in stores:
        store.wait()


def body(inputs, cotangent, weight, gain):
    micro, tokens, width = inputs.shape
    total = micro * tokens
    share = width // lax.axis_size("dp")
    window = 4 * share
    count = total // CHUNK
    vmem, dma = pltpu.VMEM, pltpu.SemaphoreType.DMA
    anywhere = pl.BlockSpec(memory_space=pl.ANY)
    shapes = (
        jax.ShapeDtypeStruct((total, width), BF16),
        jax.ShapeDtypeStruct((total, width), BF16),
        jax.ShapeDtypeStruct((share, width), F32),
    )
    results = pl.pallas_call(
        kernel,
        out_shape=shapes,
        in_specs=[anywhere] * 3 + [pl.BlockSpec(memory_space=vmem)],
        out_specs=[anywhere] * 3,
        scratch_shapes=[
            vmem((width, width), BF16),
            vmem((width, width), BF16),
            vmem((total, width), BF16),
            vmem((total, width), BF16),
            vmem((total, width), BF16),
            vmem((total, width), BF16),
            vmem((total, width), F32),
            vmem((total, 128), F32),
            vmem((2 * CHUNK, width), F32),
            vmem((total, width), BF16),
            vmem((4 * total, width), BF16),
            vmem((width, 4 * total), BF16),
            vmem((4 * total, window), BF16),
            vmem((2, 4, share, window), F32),
            vmem((2, 4, share, window), BF16),
            vmem((2, 4, share, window), BF16),
            vmem((4, share, window), BF16),
            vmem((4, share, window), BF16),
            vmem((3, share, window), BF16),
            vmem((3, share, window), BF16),
            vmem((share, width), F32),
            dma((PIECES,)),
            dma((3, count)),
            dma((2, count)),
            dma((count, PIECES)),
            dma((count, PIECES)),
            dma((count, PIECES)),
            dma((count, PIECES)),
            dma((3, count)),
            dma((3, count)),
            dma((3, count)),
            dma((3, count)),
            dma((2, 4)),
            dma((2, 4)),
            dma((4, 2)),
            dma((4, 2)),
            dma((3, 2)),
            dma((3, 2)),
        ],
        compiler_params=pltpu.CompilerParams(
            collective_id=0, has_side_effects=True, vmem_limit_bytes=62 * 1024 * 1024
        ),
    )(inputs.reshape(total, width), cotangent.reshape(total, width), weight[0], gain)
    acts, grads, wgrad = pl.pallas_call(
        place,
        out_shape=shapes,
        in_specs=[anywhere] * 3,
        out_specs=[anywhere] * 3,
        scratch_shapes=[vmem((2, total, width), BF16), vmem((share, width), F32), dma((3, 4)), dma((3, 4))],
        compiler_params=pltpu.CompilerParams(vmem_limit_bytes=62 * 1024 * 1024),
    )(*results)
    shape = (1, micro, tokens, width)
    return (acts.reshape(shape), grads.reshape(shape), wgrad[None])


def solution(mesh):
    in_specs = (
        P(None, "dp", None),
        P(None, "dp", None),
        P("section", None, None),
        P("section", None),
    )
    out_specs = (
        P("section", None, "dp", None),
        P("section", None, "dp", None),
        P("section", "dp", None),
    )
    return jax.shard_map(body, mesh=mesh, in_specs=in_specs, out_specs=out_specs, check_vma=False)
```

```python
import jax
import jax.numpy as jnp
from jax import lax
from jax.experimental import pallas as pl
from jax.experimental.pallas import tpu as pltpu
from jax.sharding import PartitionSpec as P

EPS = 1e-05
MESH = pl.DeviceIdType.MESH
BF16, F32 = jnp.bfloat16, jnp.float32

CHUNK = 16
EDGES = (0, 256, 768, 1280, 1792, 2304, 2560)
PIECES = len(EDGES) - 1
GROUP = 64
PAIRED = 2
SINGLES = 2
AHEAD = 3
BLOCKS = ((0, 1), (2, 3, 4, 5))
PADDED = 128


def kernel(
    x_hbm, d_hbm, w_hbm, gain, acts_out, grads_out, wgrad_out,
    w_v, wt_v, xs, ds_in, acts, grads, pre, rinv, acc, slopes, nx, nt, sx, partial,
    to_twin, from_twin, to_across, from_across, to_x, from_x, wgrad,
    w_sem, out_sem, home_sem, f_send, f_recv, b_send, b_recv, n_send, n_recv, s_send, s_recv,
    t_send, t_recv, y_send, y_recv, o_send, o_recv,
):
    total, width = xs.shape
    count = total // CHUNK
    window = sx.shape[1]
    share = wgrad.shape[0]
    per_group = GROUP // CHUNK
    groups = total // GROUP
    deep = 4 * GROUP
    section, dp = lax.axis_index("section"), lax.axis_index("dp")
    sections = lax.axis_size("section")
    x, y, core = dp // 4, (dp // 2) % 2, dp % 2
    first, last = section == 0, section == sections - 1
    early = section >= sections // 2

    def at(x_to, y_to, core_to):
        return (section, x_to * 4 + y_to * 2 + core_to)

    twin, across = at(x, y, 1 - core), at(x, 1 - y, core)
    odd = section % 2 == 1
    after, before = (section + 1, across[1]), (section - 1, across[1])
    steps = (1, 3, 2)
    others = [(x + step) % 4 for step in steps]

    def local(source, target, sem):
        return pltpu.make_async_copy(source, target, sem)

    def remote(source, target, send, recv, device):
        return pltpu.make_async_remote_copy(
            src_ref=source, dst_ref=target, send_sem=send, recv_sem=recv, device_id=device, device_id_type=MESH
        )

    def cols(p):
        return slice(EDGES[p], EDGES[p + 1])

    def rows_of(m, n=1):
        return pl.ds(pl.multiple_of(m * CHUNK, CHUNK), n * CHUNK)

    def slot(m, source, n=1):
        start = (m // per_group) * deep + source * GROUP + (m % per_group) * CHUNK
        return pl.ds(pl.multiple_of(start, CHUNK), n * CHUNK)

    def window_of(owner):
        return pl.ds(pl.multiple_of(owner * window, 128), window)

    def fetch_x(m):
        for p in range(PIECES):
            here = (rows_of(m), cols(p))
            local(x_hbm.at[here], xs.at[here], f_recv.at[m, p]).start()

    def fetch_d(m):
        for p in range(PIECES):
            here = (rows_of(m), cols(p))
            yield remote(d_hbm.at[here], ds_in.at[here], f_send.at[m, p], b_recv.at[m, p], across)

    def fetch_w(p):
        return local(w_hbm.at[cols(p), :], w_v.at[cols(p), :], w_sem.at[p])

    def push_acts(m, p):
        here = (rows_of(m), cols(p))
        return remote(acts.at[here], xs.at[here], f_send.at[m, p], f_recv.at[m, p], after)

    def push_grads(m, p):
        here = (rows_of(m), cols(p))
        return remote(grads.at[here], ds_in.at[here], b_send.at[m, p], b_recv.at[m, p], before)

    def push_normed(m, k):
        here = nx.at[slot(m, x), :]
        return remote(here, here, n_send.at[k, m], n_recv.at[k, m], at(others[k], y, core))

    def push_s(m, k):
        return remote(
            slopes.at[rows_of(m), window_of(others[k])],
            sx.at[slot(m, x), :],
            s_send.at[k, m],
            s_recv.at[k, m],
            at(others[k], y, core),
        )

    def keep(k, m):
        source, target = ((acts, acts_out), (grads, grads_out))[k]
        return local(source.at[rows_of(m), :], target.at[rows_of(m), :], out_sem.at[k, m])

    def home(k, m):
        source, target = ((acts, acts_out), (grads, grads_out))[k]
        return remote(
            source.at[rows_of(m), :], target.at[rows_of(m), :], out_sem.at[k, m], home_sem.at[k, m], across
        )

    def leave(k, m):
        @pl.when(odd)
        def _():
            home(k, m).start()

        @pl.when(jnp.logical_not(odd))
        def _():
            keep(k, m).start()

    @pl.when(first)
    def _():
        fetch_x(0)

    for p in range(PIECES):
        fetch_w(p).start()

    @pl.when(first)
    def _():
        fetch_x(1)

    barrier = pltpu.get_barrier_semaphore()
    for device in [twin, across] + [at(other, y, core) for other in others]:
        pl.semaphore_signal(barrier, inc=1, device_id=device, device_id_type=MESH)

    @pl.when(section > 0)
    def _():
        pl.semaphore_signal(barrier, inc=1, device_id=before, device_id_type=MESH)

    @pl.when(section < sections - 1)
    def _():
        pl.semaphore_signal(barrier, inc=1, device_id=after, device_id_type=MESH)

    pl.semaphore_wait(barrier, 5 + (section > 0).astype(jnp.int32) + (section < sections - 1).astype(jnp.int32))

    @pl.when(last)
    def _():
        @pl.loop(0, count)
        def _(m):
            for copy in fetch_d(m):
                copy.start()

    def turn_weight():
        tile = 256

        @pl.loop(0, width // tile)
        def _(i):
            i = pl.ds(pl.multiple_of(i * tile, tile), tile)
            for j in range(0, width, tile):
                wt_v[j : j + tile, i] = w_v[i, j : j + tile].T

    def turn_normed():
        for k in range(3):

            @pl.loop(0, count)
            def _(m):
                push_normed(m, k).wait_recv()

        tile = 256

        @pl.loop(0, width // tile)
        def _(i):
            i = pl.ds(pl.multiple_of(i * tile, tile), tile)
            for g in range(groups):
                g = slice(g * deep, (g + 1) * deep)
                nt[i, g] = nx[g, i].T

    def await_group(g):
        for k in range(3):
            for i in range(per_group):
                push_s(g * per_group + i, k).wait_recv()

    @pl.when(jnp.logical_not(first))
    def _():
        for p in range(PIECES):
            fetch_w(p).wait()

    @pl.when(early)
    def _():
        turn_weight()

    def add_product(lhs, rhs, p, taken):
        tile = 512
        if taken > CHUNK:
            lhs = jnp.concatenate([lhs, jnp.zeros((PADDED - taken, lhs.shape[1]), BF16)], 0)
        for j in range(0, width, tile):
            term = jnp.dot(lhs, rhs[cols(p), j : j + tile], preferred_element_type=F32)[:taken]
            if p == 0:
                acc[:taken, j : j + tile] = term
            else:
                acc[:taken, j : j + tile] += term

    def lane_sum(values):
        out = values[:, :128]
        for j in range(128, values.shape[1], 128):
            out = out + values[:, j : j + 128]
        return out

    def forward(m, n, cold=False):
        rows = rows_of(m, n)
        taken = n * CHUNK
        squares = None
        for p in range(PIECES):

            for i in range(n):
                here = xs.at[rows_of(m + i), cols(p)]
                local(here, here, f_recv.at[m + i, p]).wait()
            if cold:
                fetch_w(p).wait()
            xf = xs[rows, cols(p)].astype(F32)
            term = lane_sum(xf * xf)
            squares = term if squares is None else squares + term
            add_product((xf * gain[:, cols(p)]).astype(BF16), w_v, p, taken)
        r = lax.rsqrt(jnp.sum(squares, -1, keepdims=True) * (1.0 / width) + EPS)
        for block in BLOCKS:
            for p in block:
                a = acc[:taken, cols(p)] * r
                pre[rows, cols(p)] = a
                acts[rows, cols(p)] = (xs[rows, cols(p)].astype(F32) + a * jax.nn.sigmoid(a)).astype(BF16)

            @pl.when(section < sections - 1)
            def _():
                for i in range(n):
                    for p in block:
                        push_acts(m + i, p).start()

        if n == 1:

            @pl.when(jnp.logical_and(first, m + 2 < count))
            def _():
                fetch_x(m + 2)

        rinv[rows, :] = jnp.broadcast_to(r, (taken, 128))
        for p in range(PIECES):
            nx[slot(m, x, n), cols(p)] = (xs[rows, cols(p)].astype(F32) * r * gain[:, cols(p)]).astype(BF16)
        for i in range(n):
            leave(0, m + i)
            for k in range(3):
                push_normed(m + i, k).start()

    def backward(m, n, eager=False):
        rows = rows_of(m, n)
        taken = n * CHUNK
        dots = None
        for p in range(PIECES):
            a = pre[rows, cols(p)]
            sig = jax.nn.sigmoid(a)
            slope = sig * (1.0 + a * (1.0 - sig))

            for i in range(n):
                here = ds_in.at[rows_of(m + i), cols(p)]
                local(here, here, b_recv.at[m + i, p]).wait()
            s = (ds_in[rows, cols(p)].astype(F32) * slope).astype(BF16)
            slopes[rows, cols(p)] = s
            term = lane_sum(s.astype(F32) * a)
            dots = term if dots is None else dots + term
            if not eager:
                add_product(s, wt_v, p, taken)

        def share_s():
            for i in range(n):
                for k in range(3):
                    push_s(m + i, k).start()

        if eager:
            share_s()
            for p in range(PIECES):
                add_product(slopes[rows, cols(p)], wt_v, p, taken)
        r = rinv[rows, :1]
        scale = r * r * (jnp.sum(dots, -1, keepdims=True) * (1.0 / width))
        for block in BLOCKS:
            for p in block:
                out = (
                    ds_in[rows, cols(p)].astype(F32)
                    + r * (gain[:, cols(p)] * acc[:taken, cols(p)])
                    - xs[rows, cols(p)].astype(F32) * scale
                )
                grads[rows, cols(p)] = out.astype(BF16)

            if not eager:

                @pl.when(section > 0)
                def _():
                    for i in range(n):
                        for p in block:
                            push_grads(m + i, p).start()

        if not eager:
            share_s()
        sx[slot(m, x, n), :] = slopes[rows, window_of(x)]
        for i in range(n):
            leave(1, m + i)

    behind = sections - 1 - section
    paired = behind < PAIRED
    pairs = (count - 2 * SINGLES) // 2
    lag = jnp.where(paired, AHEAD * behind, count)

    def visit(step, work, skip, spare):
        inside = jnp.logical_and(step >= SINGLES, step < SINGLES + pairs)
        two = jnp.logical_and(paired, inside)
        start = jnp.where(step < SINGLES, step, jnp.where(inside, 2 * step - SINGLES, step + pairs))
        start = jnp.where(paired, start, step)
        active = jnp.logical_and(step >= skip, step < jnp.where(paired, pairs + 2 * SINGLES, count) - spare)

        @pl.when(jnp.logical_and(active, two))
        def _():
            work(start, 2)

        @pl.when(jnp.logical_and(active, jnp.logical_not(two)))
        def _():
            work(start, 1)

    @pl.when(first)
    def _():
        forward(0, 1, cold=True)

    @pl.loop(0, 2 * count)
    def _(i):
        visit(i, forward, first.astype(jnp.int32), 0)

        @pl.when(jnp.logical_and(i == count - 1, jnp.logical_not(early)))
        def _():
            turn_weight()
            turn_normed()

        visit(i - lag, backward, 0, first.astype(jnp.int32))

    @pl.when(first)
    def _():
        backward(count - 1, 1, eager=True)

    @pl.when(early)
    def _():
        turn_normed()

    def owner(k):
        step = jnp.where(k == 0, 2, jnp.where(k == 1, 1, jnp.where(k == 2, 3, 0)))
        return (x + step) % 4

    def product(k, y_to, core_to, tokens):
        start = owner(k) * (4 * share) + (y_to * 2 + core_to) * share
        rows = pl.ds(pl.multiple_of(start, 32), share)
        return jnp.dot(nt[rows, tokens], sx[tokens, :], preferred_element_type=F32)

    known, tail = slice(0, (groups - 1) * deep), slice((groups - 1) * deep, groups * deep)
    for g in range(groups - 1):
        await_group(g)

    @pl.loop(0, 4)
    def _(k):
        partial[0, k] = product(k, 1 - y, 1 - core, known)
        partial[1, k] = product(k, 1 - y, core, known)

    await_group(groups - 1)

    def push_twin(half, k):
        return remote(to_twin.at[half, k], from_twin.at[half, k], t_send.at[half, k], t_recv.at[half, k], twin)

    half = share // 2

    def half_of(h):
        return pl.ds(pl.multiple_of(h * half, 16), half)

    def push_across(k, h):
        here = (k, half_of(h))
        return remote(to_across.at[here], from_across.at[here], y_send.at[k, h], y_recv.at[k, h], across)

    def push_owner(k, h):
        here = (k, half_of(h))
        return remote(to_x.at[here], from_x.at[here], o_send.at[k, h], o_recv.at[k, h], at(owner(k), y, core))

    def keep_wgrad(source):
        return local(wgrad.at[:, window_of(source)], wgrad_out.at[:, window_of(source)], out_sem.at[2, source])

    norm = float(4096) ** (-0.5)

    def offer(k):
        to_twin[0, k] = (partial[0, k] + product(k, 1 - y, 1 - core, tail)).astype(BF16)
        push_twin(0, k).start()

    def hand_on(k):
        value = partial[1, k] + product(k, 1 - y, core, tail)
        push_twin(0, k).wait_recv()
        to_across[k] = (value + from_twin[0, k].astype(F32)).astype(BF16)
        for h in range(2):
            push_across(k, h).start()

    pl.loop(0, 2)(offer)

    @pl.loop(0, 2)
    def _(k):
        hand_on(k)
        offer(k + 2)

    pl.loop(2, 4)(hand_on)

    @pl.loop(0, 4)
    def _(k):
        to_twin[1, k] = product(k, y, 1 - core, slice(None)).astype(BF16)
        push_twin(1, k).start()

    @pl.loop(0, 4)
    def _(k):
        value = product(k, y, core, slice(None))
        push_twin(1, k).wait_recv()
        partial[0, k] = value + from_twin[1, k].astype(F32)

    @pl.loop(0, count)
    def _(m):
        for k in range(3):
            push_normed(m, k).wait_send()
            push_s(m, k).wait_send()
        for k in range(2):

            @pl.when(odd)
            def _():
                home(k, m).wait()

            @pl.when(jnp.logical_not(odd))
            def _():
                keep(k, m).wait()

        @pl.when(last)
        def _():
            for copy in fetch_d(m):
                copy.wait_send()

        for p in range(PIECES):

            @pl.when(section < sections - 1)
            def _():
                push_acts(m, p).wait_send()

            @pl.when(section > 0)
            def _():
                push_grads(m, p).wait_send()

    @pl.loop(0, 3)
    def _(k):
        for h in range(2):
            push_across(k, h).wait_recv()
            to_x[k, half_of(h)] = (partial[0, k, half_of(h)] + from_across[k, half_of(h)].astype(F32)).astype(BF16)
            push_owner(k, h).start()

    for h in range(2):
        push_across(3, h).wait_recv()
    wgrad[:, window_of(x)] = norm * (partial[0, 3] + from_across[3].astype(F32))
    keep_wgrad(x).start()
    for k, step in enumerate((2, 3, 1)):
        source = (x + step) % 4
        for h in range(2):
            push_owner(k, h).wait_recv()
        wgrad[:, window_of(source)] = norm * from_x[k].astype(F32)
        keep_wgrad(source).start()

    @pl.loop(0, 4)
    def _(k):
        push_twin(0, k).wait_send()
        push_twin(1, k).wait_send()
        for h in range(2):
            push_across(k, h).wait_send()

    for k in range(3):
        for h in range(2):
            push_owner(k, h).wait_send()

    for k in range(4):
        keep_wgrad(k).wait()


def place(acts_in, grads_in, wgrad_in, acts, grads, wgrad, held, held_wide, in_sems, out_sems):
    parts = 4
    loads, stores = [], []
    arrays = ((acts_in, held.at[0], acts), (grads_in, held.at[1], grads), (wgrad_in, held_wide, wgrad))
    for k, (source, middle, target) in enumerate(arrays):
        step = source.shape[0] // parts
        for i in range(parts):
            rows = slice(i * step, (i + 1) * step)
            loads.append(pltpu.make_async_copy(source.at[rows, :], middle.at[rows, :], in_sems.at[k, i]))
            stores.append(pltpu.make_async_copy(middle.at[rows, :], target.at[rows, :], out_sems.at[k, i]))
    for load in loads:
        load.start()
    for load, store in zip(loads, stores):
        load.wait()
        store.start()
    for store in stores:
        store.wait()


def body(inputs, cotangent, weight, gain):
    micro, tokens, width = inputs.shape
    total = micro * tokens
    share = width // lax.axis_size("dp")
    window = 4 * share
    count = total // CHUNK
    vmem, dma = pltpu.VMEM, pltpu.SemaphoreType.DMA
    anywhere = pl.BlockSpec(memory_space=pl.ANY)
    shapes = (
        jax.ShapeDtypeStruct((total, width), BF16),
        jax.ShapeDtypeStruct((total, width), BF16),
        jax.ShapeDtypeStruct((share, width), F32),
    )
    results = pl.pallas_call(
        kernel,
        out_shape=shapes,
        in_specs=[anywhere] * 3 + [pl.BlockSpec(memory_space=vmem)],
        out_specs=[anywhere] * 3,
        scratch_shapes=[
            vmem((width, width), BF16),
            vmem((width, width), BF16),
            vmem((total, width), BF16),
            vmem((total, width), BF16),
            vmem((total, width), BF16),
            vmem((total, width), BF16),
            vmem((total, width), F32),
            vmem((total, 128), F32),
            vmem((2 * CHUNK, width), F32),
            vmem((total, width), BF16),
            vmem((4 * total, width), BF16),
            vmem((width, 4 * total), BF16),
            vmem((4 * total, window), BF16),
            vmem((2, 4, share, window), F32),
            vmem((2, 4, share, window), BF16),
            vmem((2, 4, share, window), BF16),
            vmem((4, share, window), BF16),
            vmem((4, share, window), BF16),
            vmem((3, share, window), BF16),
            vmem((3, share, window), BF16),
            vmem((share, width), F32),
            dma((PIECES,)),
            dma((3, count)),
            dma((2, count)),
            dma((count, PIECES)),
            dma((count, PIECES)),
            dma((count, PIECES)),
            dma((count, PIECES)),
            dma((3, count)),
            dma((3, count)),
            dma((3, count)),
            dma((3, count)),
            dma((2, 4)),
            dma((2, 4)),
            dma((4, 2)),
            dma((4, 2)),
            dma((3, 2)),
            dma((3, 2)),
        ],
        compiler_params=pltpu.CompilerParams(
            collective_id=0, has_side_effects=True, vmem_limit_bytes=62 * 1024 * 1024
        ),
    )(inputs.reshape(total, width), cotangent.reshape(total, width), weight[0], gain)
    acts, grads, wgrad = pl.pallas_call(
        place,
        out_shape=shapes,
        in_specs=[anywhere] * 3,
        out_specs=[anywhere] * 3,
        scratch_shapes=[vmem((2, total, width), BF16), vmem((share, width), F32), dma((3, 4)), dma((3, 4))],
        compiler_params=pltpu.CompilerParams(vmem_limit_bytes=62 * 1024 * 1024),
    )(*results)
    shape = (1, micro, tokens, width)
    return (acts.reshape(shape), grads.reshape(shape), wgrad[None])


def solution(mesh):
    in_specs = (
        P(None, "dp", None),
        P(None, "dp", None),
        P("section", None, None),
        P("section", None),
    )
    out_specs = (
        P("section", None, "dp", None),
        P("section", None, "dp", None),
        P("section", "dp", None),
    )
    return jax.shard_map(body, mesh=mesh, in_specs=in_specs, out_specs=out_specs, check_vma=False)
```
